128 devices in a mesh: row: 16 (over x, y), col: 8 (over z, core).
Axes of the slice: x: 4, y: 4, z: 4, core: 2. Of those that a mesh axis runs over, the one named last changes fastest.
Arguments:
- x_mat: float32 [512, 512], replicated, may hold values from -8 to 40, as said below
- y_inv: float32 [512, 512], replicated, may hold values from -8 to 40, as said below
- panel_blocks: bfloat16 [512, 4096], replicated, may hold values from -6 to 6
- panel_pos: int32 [512], replicated, may hold values from 0 to 63
- group_blocks: int32 [128, 2], replicated, may hold values from 0 to 63
- cons_blocks: bfloat16 [114688, 4096], P(('row', 'col')), may hold values from -6 to 6
- slot_block: int32 [114688], P(('row', 'col')), may hold values from 0 to 1
- slot_row: int32 [114688], P(('row', 'col')), may hold values from 0 to 65535, as said below
- group_size: int32 [128], P(('row', 'col')), may hold values from 384 to 896, as said below
- trailing: float32 [65536, 2048], P('row', 'col'), may hold values from -6 to 6
Outputs:
- lower_panel: float32 [65536, 512], P(('row', 'col'))
- updated: float32 [65536, 2048], P('row', 'col')
The draws below stay inside these ranges and needn't reach their ends.
Inputs may be any that keep to these rules, and one draw needn't show every extreme that they name: `x_mat`: symmetric positive definite. `y_inv`: symmetric positive definite. `slot_row`: over all groups, the live slots hold every row 0 to 65535 exactly once; the live slots of one group hold at most 7 rows of one aligned range of 512 rows, and that most is reached in every draw; other slots hold arbitrary rows. `group_size`: the live slots of a group are its first slots; some group has exactly 896 in every draw.
All inputs are finite; a program needn't handle non-finite values.
Results may differ from the reference program's by a relative error of at most 0.004.
Values may be sent and summed in bfloat16 or wider, within the bound.
No kernel may reach another device: no remote copies, remote signals or barrier semaphores. Data moves between devices by JAX's collectives and lax.ppermute only.
A program may use at most 192 MiB of HBM per device.

```python
import math
import jax
import jax.numpy as jnp
from jax import lax

N = 512
BS = 64
NB = 8
PANEL = 512
TRAIL = 2048
CAP = 2
ROWS_DEV = 4096
M2 = 65536
SUB = 512
CS = 896
RB = 16
N_ROW = 16
N_COL = 8
DEVICES = 128


def spd_matrix(key, salt):
    key_one = jax.random.fold_in(jax.random.fold_in(key, salt), 0)
    base = jax.random.normal(key_one, (N, N), jnp.float32)
    gram = jnp.dot(base, base.T, precision=lax.Precision.HIGHEST) / N
    return gram + 0.3 * jnp.eye(N, dtype=jnp.float32)


def draw_x_mat(key, part):
    return spd_matrix(key, 3)


def draw_y_inv(key, part):
    return spd_matrix(key, 5)


def slot_layout(key):
    devices = N_ROW * N_COL
    base_share = SUB // devices
    spread = SUB - devices // 4 * base_share
    key_list = jax.random.split(jax.random.fold_in(key, 11), 5)
    heavy_part = jax.random.permutation(key_list[0], jnp.where(jnp.arange(devices) < devices // 4, base_share, 0).astype(jnp.int32))
    extra_part = jax.random.permutation(key_list[1], (spread // devices + (jnp.arange(devices) < spread % devices).astype(jnp.int32)).astype(jnp.int32))
    source_ids = jnp.arange(devices)[:, None]
    dest_ids = jnp.arange(devices)[None, :]
    counts = heavy_part[:, None] + extra_part[(source_ids + dest_ids) % devices]
    recv_start = jnp.cumsum(counts, axis=0) - counts
    orders = jax.vmap(lambda sub_key: jax.random.permutation(sub_key, SUB))(jax.random.split(key_list[2], devices))
    send_end = jnp.cumsum(counts, axis=1)
    send_start = send_end - counts
    group_total = send_end[:, -1]
    slot_ids = jnp.arange(CS, dtype=jnp.int32)
    dest_of = jax.vmap(lambda ends: jnp.searchsorted(ends, slot_ids, side='right'))(send_end)
    dest_clip = jnp.minimum(dest_of, devices - 1).astype(jnp.int32)
    offset = slot_ids[None, :] - jnp.take_along_axis(send_start, dest_clip, axis=1)
    local_pos = jnp.clip(jnp.take_along_axis(recv_start, dest_clip, axis=1) + offset, 0, SUB - 1)
    local_row = orders[dest_clip, local_pos]
    live_slots = slot_ids[None, :] < group_total[:, None]
    dead_rows = jax.random.randint(key_list[3], (devices, CS), 0, M2)
    row_ids = jnp.where(live_slots, dest_clip * SUB + local_row, dead_rows)
    sort_key = jax.random.randint(key_list[4], (devices, CS), 0, 1 << 20) + jnp.where(live_slots, 0, 1 << 21)
    shuffle = jnp.argsort(sort_key, axis=1, stable=True)
    row_ids = jnp.take_along_axis(row_ids, shuffle, axis=1)
    return (row_ids.reshape(-1).astype(jnp.int32), group_total.astype(jnp.int32))


def draw_slot_row(key, part):
    return slot_layout(key)[0]


def draw_group_size(key, part):
    return slot_layout(key)[1]


def set_ends(result, rng, smallest, high):
    dims = result.shape
    place = [jax.random.randint(jax.random.fold_in(rng, axis), (), 0, dims[axis]) for axis in range(len(dims))]
    result = result.at[tuple(place)].set(smallest)
    longest = dims.index(max(dims))
    place[longest] = (place[longest] + 1) % dims[longest]
    return result.at[tuple(place)].set(high)


def block_levels(own_key, extent, cuts, smallest, high):
    def one(dim, blocks):
        heights = jax.random.uniform(jax.random.fold_in(jax.random.fold_in(own_key, 6), dim), (blocks,), jnp.float32, smallest / len(cuts), high / len(cuts))
        return jnp.repeat(jnp.exp(heights), extent[dim] // blocks).reshape((-1,) + (1,) * (len(extent) - dim - 1))

    loudness = one(*cuts[0])
    for cut in cuts[1:]:
        loudness = loudness * one(*cut)
    return loudness


def normal_values(key, shape, scale, bound, cuts=(), kind=jnp.bfloat16):
    result = jax.random.normal(key, shape, jnp.float32) * scale
    if len(cuts) > 0:
        result = block_levels(key, shape, cuts, -0.22, 0.18) * result
    return jnp.clip(result, min=-bound, max=bound).astype(kind)


def setup_inputs(seed: int = 0) -> dict:
    seeds = jax.random.split(jax.random.key(seed), 11)
    return {
        "x_mat": draw_x_mat(jax.random.fold_in(seeds[10], 71), 0),
        "y_inv": draw_y_inv(jax.random.fold_in(seeds[10], 71), 0),
        "panel_blocks": normal_values(seeds[2], (PANEL, BS * BS), 1.0, 6.0),
        "panel_pos": set_ends(jax.random.randint(seeds[3], (PANEL,), 0, NB * NB), jax.random.fold_in(seeds[3], 1), 0, (NB * NB) - 1).astype(jnp.int32),
        "group_blocks": set_ends(jax.random.randint(seeds[4], (DEVICES, CAP), 0, NB * NB), jax.random.fold_in(seeds[4], 1), 0, (NB * NB) - 1).astype(jnp.int32),
        "cons_blocks": normal_values(seeds[5], (DEVICES * CS, BS * BS), 1.0, 6.0, ((0, 128),)),
        "slot_block": set_ends(jax.random.randint(seeds[6], (DEVICES * CS,), 0, CAP), jax.random.fold_in(seeds[6], 1), 0, CAP - 1).astype(jnp.int32),
        "slot_row": draw_slot_row(jax.random.fold_in(seeds[10], 71), 0),
        "group_size": draw_group_size(jax.random.fold_in(seeds[10], 71), 0),
        "trailing": normal_values(seeds[9], (M2, TRAIL), 1.0, 6.0, ((0, 16), (1, 8)), jnp.float32),
    }


def build_h(values, position, x_mat, y_inv):
    highest = lax.Precision.HIGHEST
    matrix_order = x_mat.shape[0]
    block_size = math.isqrt(values.shape[0])
    block_count = matrix_order // block_size
    e_mat = values.reshape(block_size, block_size).astype(jnp.float32)
    row_start = position // block_count * block_size
    col_start = position % block_count * block_size
    x_left = lax.dynamic_slice_in_dim(x_mat, row_start, block_size, 1)
    x_right = lax.dynamic_slice_in_dim(x_mat, col_start, block_size, 1)
    y_low = lax.dynamic_slice_in_dim(y_inv, col_start, block_size, 0)
    y_high = lax.dynamic_slice_in_dim(y_inv, row_start, block_size, 0)
    term_one = jnp.dot(jnp.dot(x_left, e_mat, precision=highest), y_low, precision=highest)
    term_two = jnp.dot(jnp.dot(x_right, e_mat.T, precision=highest), y_high, precision=highest)
    g_mat = term_one + term_two
    h_mat = (g_mat + g_mat.T).astype(jnp.bfloat16)
    h_mat = h_mat.reshape(block_count, block_size, block_count, block_size).transpose(0, 2, 1, 3)
    return h_mat.reshape(block_count * block_count, block_size * block_size)

def reference(x_mat, y_inv, panel_blocks, panel_pos, group_blocks, cons_blocks, slot_block, slot_row, group_size, trailing):
    highest = lax.Precision.HIGHEST
    devices = N_ROW * N_COL
    blocks_all = lax.map(lambda pair_item: build_h(pair_item[0], pair_item[1], x_mat, y_inv), (panel_blocks, panel_pos))
    panel_float = panel_blocks.astype(jnp.float32)

    def diag_column(blocks_one):
        chosen = jnp.take(blocks_one, panel_pos, axis=0).astype(jnp.float32)
        return lax.optimization_barrier(jnp.sum(panel_float * chosen, axis=1))
    panel_schur = lax.map(diag_column, blocks_all).T
    symmetric = 0.5 * (panel_schur + panel_schur.T)
    diag_shift = 0.01 * jnp.mean(jnp.diagonal(symmetric))
    factor = jnp.linalg.cholesky(symmetric + diag_shift * jnp.eye(PANEL, dtype=jnp.float32))

    def device_rows(dev_item):
        cons_dev, blocks_dev, which_dev = dev_item
        cons_float = cons_dev.astype(jnp.float32)
        running = jnp.zeros((CS, PANEL), jnp.float32)
        for slot_index in range(CAP):
            table = jnp.take(blocks_all, blocks_dev[slot_index], axis=1).astype(jnp.float32)
            product_part = jnp.dot(cons_float, table.T, precision=highest)
            running = jnp.where((which_dev == slot_index)[:, None], product_part, running)
        return running
    rows_all = lax.map(device_rows, (cons_blocks.reshape(devices, CS, BS * BS), group_blocks, slot_block.reshape(devices, CS)))
    live_slots = jnp.arange(CS, dtype=jnp.int32)[None, :] < group_size[:, None]
    target = jnp.where(live_slots, slot_row.reshape(devices, CS), M2).astype(jnp.int32)
    row_schur = jnp.zeros((M2, PANEL), jnp.float32).at[target.reshape(-1)].set(rows_all.reshape(-1, PANEL), mode='drop')
    lower_panel = lax.linalg.triangular_solve(factor, row_schur, left_side=False, lower=True, transpose_a=True)
    col_ids = jnp.arange(TRAIL, dtype=jnp.int32)
    source = col_ids // RB % N_ROW * ROWS_DEV + col_ids // (RB * N_ROW) * RB + col_ids % RB
    picked = jnp.take(lower_panel, source.astype(jnp.int32), axis=0)
    updated = trailing - jnp.dot(lower_panel, picked.T, precision=highest)
    return (lower_panel, updated)
```

```python
import functools

import jax
import jax.numpy as jnp
from jax import lax
from jax.experimental import pallas as pl
from jax.experimental.pallas import tpu as pltpu
from jax.sharding import PartitionSpec as P

F32 = jnp.float32
BF16 = jnp.bfloat16
BS = 64
NB = 8
N = 512
AXES = ("row", "col")
NT = (((1,), (1,)), ((), ()))
TN = (((0,), (0,)), ((), ()))


def split(a):
    high = a.astype(BF16)
    return high, (a - high.astype(F32)).astype(BF16)


def split_outside(a):
    high = lax.reduce_precision(a, 8, 7)
    return high.astype(BF16), (a - high).astype(BF16)


def dot(a, b, dims=(((1,), (0,)), ((), ()))):
    return lax.dot_general(a, b, dims, preferred_element_type=F32)


def panel_kernel(pos_ref, x_ref, y_ref, e_ref, panel_ref, rowid_ref, t_ref, ps_ref, h_ref, f_ref):
    count = e_ref.shape[0]
    lane = lax.broadcasted_iota(jnp.int32, (8, 128), 1)
    for j in range(count):
        position = pos_ref[j]
        p = pl.multiple_of(position // NB * BS, BS)
        q = pl.multiple_of(position % NB * BS, BS)
        e = e_ref[j].astype(F32)
        highest = lax.Precision.HIGHEST
        ey = jnp.dot(e, y_ref[pl.ds(q, BS), :], precision=highest, preferred_element_type=F32)
        ety = jnp.dot(e.T, y_ref[pl.ds(p, BS), :], precision=highest, preferred_element_type=F32)
        xh, xl = split(jnp.concatenate([x_ref[pl.ds(p, BS), :], x_ref[pl.ds(q, BS), :]], 0))
        vh, vl = split(jnp.concatenate([ey, ety], 0))
        ah = jnp.concatenate([xh, vh], 0)
        al = jnp.concatenate([xl, vl], 0)
        bh = jnp.concatenate([vh, xh], 0)
        bl = jnp.concatenate([vl, xl], 0)
        h = dot(ah, bh, TN) + (dot(ah, bl, TN) + dot(al, bh, TN))
        for b in range(NB // 2):
            h_ref[b] = h[:, b * 128 : b * 128 + 128]

        def relayout(pair, carry):
            r = pair * 2
            out = pl.ds(pl.multiple_of(pair * 128, 128), 128)
            for b in range(NB // 2):
                u = h_ref[b, pl.ds(r, NB, stride=BS), :]
                v = h_ref[b, pl.ds(r + 1, NB, stride=BS), :]
                f_ref[16 * b : 16 * b + 8, out] = jnp.where(lane < BS, u, pltpu.roll(v, BS, 1))
                f_ref[16 * b + 8 : 16 * b + 16, out] = jnp.where(lane < BS, pltpu.roll(u, BS, 1), v)
            return carry

        lax.fori_loop(0, BS // 2, relayout, 0, unroll=4)
        t_ref[j * 64 : j * 64 + 64, :] = f_ref[...].astype(BF16)
    hit = lax.broadcasted_iota(jnp.int32, (NB * NB, N), 0) == rowid_ref[...]
    for j in range(count):
        all_blocks = dot(t_ref[j * 64 : j * 64 + 64, :], panel_ref[...], NT)
        ps_ref[j : j + 1, :] = jnp.sum(jnp.where(hit, all_blocks, 0.0), axis=0, keepdims=True)


def panel_call(own_pos, x_mat, y_inv, own_e, panel_blocks, row_ids):
    count = own_e.shape[0]
    vmem = pl.BlockSpec(memory_space=pltpu.VMEM)
    return pl.pallas_call(
        panel_kernel,
        out_shape=(
            jax.ShapeDtypeStruct((count * NB * NB, BS * BS), BF16),
            jax.ShapeDtypeStruct((count, N), F32),
        ),
        in_specs=[pl.BlockSpec(memory_space=pltpu.SMEM)] + [vmem] * 5,
        out_specs=(vmem, vmem),
        scratch_shapes=[pltpu.VMEM((NB // 2, N, 2 * BS), F32), pltpu.VMEM((NB * NB, BS * BS), F32)],
        compiler_params=pltpu.CompilerParams(vmem_limit_bytes=40 * 2**20),
        name="panel",
    )(own_pos, x_mat, y_inv, own_e, panel_blocks, row_ids)


def row_id(position):
    return position % NB * NB + position // NB


def body(
    x_mat,
    y_inv,
    panel_blocks,
    panel_pos,
    group_blocks,
    cons_blocks,
    slot_block,
    slot_row,
    group_size,
    trailing,
):
    rows_size = lax.axis_size("row")
    cols_size = lax.axis_size("col")
    devices = rows_size * cols_size
    col_index = lax.axis_index("col")
    device_id = lax.axis_index("row") * cols_size + col_index
    panel_cols = panel_blocks.shape[0]
    own = panel_cols // devices
    slots = cons_blocks.shape[0]
    sub_rows = trailing.shape[0] // cols_size
    places = 8

    live = jnp.arange(slots, dtype=jnp.int32) < group_size[0]
    target = slot_row // sub_rows
    hits = ((target[:, None] == jnp.arange(devices, dtype=jnp.int32)[None, :]) & live[:, None]).astype(BF16)
    earlier = (
        lax.broadcasted_iota(jnp.int32, (slots, slots), 0) > lax.broadcasted_iota(jnp.int32, (slots, slots), 1)
    ).astype(BF16)
    rank = jnp.sum(dot(earlier, hits) * hits.astype(F32), axis=1).astype(jnp.int32)
    place = jnp.where(live, target * places + rank, -1)
    sends = lax.broadcasted_iota(jnp.int32, (devices * places, slots), 0) == place[None, :]
    local = jnp.sum(jnp.where(sends, (slot_row % sub_rows + 1)[None, :], 0), axis=1)
    local = lax.all_to_all(local.reshape(devices, places), AXES, 0, 0, tiled=True).reshape(-1) - 1
    sends = sends.astype(BF16)
    puts = (lax.broadcasted_iota(jnp.int32, (sub_rows, devices * places), 0) == local[None, :]).astype(BF16)

    own_values = lax.dynamic_slice_in_dim(panel_blocks, device_id * own, own, 0).reshape(own, BS, BS)
    own_pos = lax.dynamic_slice_in_dim(panel_pos, device_id * own, own, 0)
    flat, ps_rows = panel_call(own_pos, x_mat, y_inv, own_values, panel_blocks, row_id(panel_pos)[None, :])
    ps = lax.all_to_all(jnp.broadcast_to(ps_rows[None], (devices, own, panel_cols)), AXES, 0, 0, tiled=True)
    ps = ps.reshape(panel_cols, panel_cols)

    wanted = jnp.broadcast_to(row_id(group_blocks)[:, :, None], (devices, 2, own)) + jnp.arange(own) * NB * NB
    pick = (wanted.reshape(-1)[:, None] == jnp.arange(own * NB * NB)[None, :]).astype(BF16)
    outgoing = dot(pick, flat).astype(BF16)
    outgoing, ps = lax.optimization_barrier((outgoing, ps))
    blocks = lax.all_to_all(outgoing.reshape(devices, 2 * own, BS * BS), AXES, 0, 0, tiled=True)
    blocks = blocks.reshape(devices * 2 * own, BS * BS)

    symmetric = 0.5 * (ps + ps.T)
    shift = 0.01 * jnp.mean(jnp.diagonal(symmetric))
    eye = jnp.eye(panel_cols, dtype=F32)
    factor = jnp.linalg.cholesky(symmetric + shift * eye)
    inverse_t = lax.linalg.triangular_solve(factor, eye, left_side=False, lower=True, transpose_a=True)
    inverse_t = jnp.broadcast_to(
        inverse_t.reshape(devices, 1, own, panel_cols), (devices, 2, own, panel_cols)
    ).reshape(devices * 2 * own, panel_cols)

    product = dot(cons_blocks, blocks, NT)
    which = (jnp.arange(devices * 2 * own) // own) % 2
    product = jnp.where(slot_block[:, None] == which[None, :], product, 0.0)
    ph, plo = split_outside(product)
    ih, ilo = split_outside(inverse_t)
    lower = dot(ph, ih) + (dot(ph, ilo) + dot(plo, ih))
    lh, llo = split_outside(lower)
    send = dot(sends, lh) + dot(sends, llo)
    recv = lax.all_to_all(send.reshape(devices, places, panel_cols), AXES, 0, 0, tiled=True)
    rh, rlo = split_outside(recv.reshape(devices * places, panel_cols))
    slab_high = dot(puts, rh)
    lower_slab = slab_high + dot(puts, rlo)
    slab_high = slab_high.astype(BF16)

    block_rows = trailing.shape[1] // rows_size
    lead = lax.all_to_all(slab_high[: block_rows * cols_size].reshape(cols_size, block_rows, panel_cols), "col", 0, 0, tiled=True)[0]
    picked = lax.all_to_all(jnp.broadcast_to(lead[None], (rows_size, block_rows, panel_cols)), "row", 0, 0, tiled=True)
    picked = picked.reshape(trailing.shape[1], panel_cols)
    all_rows = lax.all_gather(slab_high, "col", axis=0, tiled=True)
    updated = trailing - dot(all_rows, picked, NT)
    return (lower_slab, updated)


def solution(mesh):
    return jax.shard_map(
        body,
        mesh=mesh,
        in_specs=(
            P(),
            P(),
            P(),
            P(),
            P(),
            P(("row", "col"), None),
            P(("row", "col")),
            P(("row", "col")),
            P(("row", "col")),
            P("row", "col"),
        ),
        out_specs=(P(("row", "col"), None), P("row", "col")),
        check_vma=False,
    )
```

```python
import functools

import jax
import jax.numpy as jnp
from jax import lax
from jax.experimental import pallas as pl
from jax.experimental.pallas import tpu as pltpu
from jax.sharding import PartitionSpec as P

F32 = jnp.float32
BF16 = jnp.bfloat16
BS = 64
NB = 8
N = 512
AXES = ("row", "col")
NT = (((1,), (1,)), ((), ()))
TN = (((0,), (0,)), ((), ()))


def split(a):
    high = a.astype(BF16)
    return high, (a - high.astype(F32)).astype(BF16)


def split_outside(a):
    high = lax.reduce_precision(a, 8, 7)
    return high.astype(BF16), (a - high).astype(BF16)


def dot(a, b, dims=(((1,), (0,)), ((), ()))):
    return lax.dot_general(a, b, dims, preferred_element_type=F32)


def panel_kernel(pos_ref, x_ref, y_ref, e_ref, panel_ref, rowid_ref, t_ref, ps_ref, h_ref, f_ref):
    count = e_ref.shape[0]
    lane = lax.broadcasted_iota(jnp.int32, (8, 128), 1)
    for j in range(count):
        position = pos_ref[j]
        p = pl.multiple_of(position // NB * BS, BS)
        q = pl.multiple_of(position % NB * BS, BS)
        e = e_ref[j].astype(F32)
        highest = lax.Precision.HIGHEST
        ey = jnp.dot(e, y_ref[pl.ds(q, BS), :], precision=highest, preferred_element_type=F32)
        ety = jnp.dot(e.T, y_ref[pl.ds(p, BS), :], precision=highest, preferred_element_type=F32)
        xh, xl = split(jnp.concatenate([x_ref[pl.ds(p, BS), :], x_ref[pl.ds(q, BS), :]], 0))
        vh, vl = split(jnp.concatenate([ey, ety], 0))
        ah = jnp.concatenate([xh, vh], 0)
        al = jnp.concatenate([xl, vl], 0)
        bh = jnp.concatenate([vh, xh], 0)
        bl = jnp.concatenate([vl, xl], 0)
        h = dot(ah, bh, TN) + (dot(ah, bl, TN) + dot(al, bh, TN))
        for b in range(NB // 2):
            h_ref[b] = h[:, b * 128 : b * 128 + 128]

        def relayout(pair, carry):
            r = pair * 2
            out = pl.ds(pl.multiple_of(pair * 128, 128), 128)
            for b in range(NB // 2):
                u = h_ref[b, pl.ds(r, NB, stride=BS), :]
                v = h_ref[b, pl.ds(r + 1, NB, stride=BS), :]
                f_ref[16 * b : 16 * b + 8, out] = jnp.where(lane < BS, u, pltpu.roll(v, BS, 1))
                f_ref[16 * b + 8 : 16 * b + 16, out] = jnp.where(lane < BS, pltpu.roll(u, BS, 1), v)
            return carry

        lax.fori_loop(0, BS // 2, relayout, 0, unroll=4)
        t_ref[j * 64 : j * 64 + 64, :] = f_ref[...].astype(BF16)
    hit = lax.broadcasted_iota(jnp.int32, (NB * NB, N), 0) == rowid_ref[...]
    for j in range(count):
        all_blocks = dot(t_ref[j * 64 : j * 64 + 64, :], panel_ref[...], NT)
        ps_ref[j : j + 1, :] = jnp.sum(jnp.where(hit, all_blocks, 0.0), axis=0, keepdims=True)


def panel_call(own_pos, x_mat, y_inv, own_e, panel_blocks, row_ids):
    count = own_e.shape[0]
    vmem = pl.BlockSpec(memory_space=pltpu.VMEM)
    return pl.pallas_call(
        panel_kernel,
        out_shape=(
            jax.ShapeDtypeStruct((count * NB * NB, BS * BS), BF16),
            jax.ShapeDtypeStruct((count, N), F32),
        ),
        in_specs=[pl.BlockSpec(memory_space=pltpu.SMEM)] + [vmem] * 5,
        out_specs=(vmem, vmem),
        scratch_shapes=[pltpu.VMEM((NB // 2, N, 2 * BS), F32), pltpu.VMEM((NB * NB, BS * BS), F32)],
        compiler_params=pltpu.CompilerParams(vmem_limit_bytes=40 * 2**20),
        name="panel",
    )(own_pos, x_mat, y_inv, own_e, panel_blocks, row_ids)


def factor_kernel(ps_ref, inv_ref, s_ref):
    order = ps_ref.shape[0]
    wide = 128
    highest = lax.Precision.HIGHEST
    ps = ps_ref[...]
    diagonal = lax.broadcasted_iota(jnp.int32, (order, order), 0) == lax.broadcasted_iota(jnp.int32, (order, order), 1)
    symmetric = 0.5 * (ps + ps.T)
    trace = jnp.sum(jnp.sum(jnp.where(diagonal, symmetric, 0.0), axis=1, keepdims=True), axis=0, keepdims=True)
    s_ref[...] = symmetric + jnp.where(diagonal, 0.01 / order * trace, 0.0)
    inv_ref[...] = jnp.where(diagonal, 1.0, 0.0)
    sub = lax.broadcasted_iota(jnp.int32, (8, wide), 0)
    small = lax.broadcasted_iota(jnp.int32, (wide, wide), 0) == lax.broadcasted_iota(jnp.int32, (wide, wide), 1)
    tiles = wide // 8
    for block in range(order // wide):
        at = slice(block * wide, block * wide + wide)
        whole = s_ref[at, at]
        a = [whole[8 * t : 8 * t + 8, :] for t in range(tiles)]
        w = [jnp.where(small[8 * t : 8 * t + 8, :], 1.0, 0.0) for t in range(tiles)]
        for m in range(tiles):
            cols = {
                t: [jnp.broadcast_to(a[t][:, 8 * m + c : 8 * m + c + 1], (8, wide)) for c in range(8)]
                for t in range(m, tiles)
            }
            scale = jnp.zeros((8, wide), F32)
            for c in range(8):
                pivot = jnp.broadcast_to(cols[m][c][c : c + 1, :], (8, wide))
                root = lax.rsqrt(pivot)
                root = root * (1.5 - 0.5 * pivot * root * root)
                scale = jnp.where(sub == c, root, scale)
                less = root * root
                row_a = jnp.broadcast_to(a[m][c : c + 1, :], (8, wide))
                row_w = jnp.broadcast_to(w[m][c : c + 1, :], (8, wide))
                heads = [jnp.broadcast_to(cols[m][d][c : c + 1, :], (8, wide)) for d in range(c + 1, 8)]
                for t in range(m, tiles):
                    times = cols[t][c] * less
                    if t == m:
                        times = jnp.where(sub > c, times, 0.0)
                    a[t] = a[t] - times * row_a
                    w[t] = w[t] - times * row_w
                    for d in range(c + 1, 8):
                        cols[t][d] = cols[t][d] - times * heads[d - c - 1]
            w[m] = w[m] * scale
        low = jnp.concatenate(w, 0)
        row_inv = jnp.dot(low, inv_ref[at, :], precision=highest, preferred_element_type=F32)
        inv_ref[at, :] = row_inv
        if (block + 1) * wide < order:
            rest = slice((block + 1) * wide, order)
            row_s = jnp.dot(low, s_ref[at, rest], precision=highest, preferred_element_type=F32)
            s_ref[rest, rest] -= lax.dot_general(row_s, row_s, TN, precision=highest, preferred_element_type=F32)
            inv_ref[rest, :] -= lax.dot_general(row_s, row_inv, TN, precision=highest, preferred_element_type=F32)


def factor_call(ps):
    vmem = pl.BlockSpec(memory_space=pltpu.VMEM)
    return pl.pallas_call(
        factor_kernel,
        out_shape=jax.ShapeDtypeStruct(ps.shape, F32),
        in_specs=[vmem],
        out_specs=vmem,
        scratch_shapes=[pltpu.VMEM(ps.shape, F32)],
        compiler_params=pltpu.CompilerParams(vmem_limit_bytes=32 * 2**20),
        cost_estimate=pl.CostEstimate(flops=4 * 10**9, bytes_accessed=4 * 2**20, transcendentals=0),
        name="factor",
    )(ps)


def row_id(position):
    return position % NB * NB + position // NB


def body(
    x_mat,
    y_inv,
    panel_blocks,
    panel_pos,
    group_blocks,
    cons_blocks,
    slot_block,
    slot_row,
    group_size,
    trailing,
):
    rows_size = lax.axis_size("row")
    cols_size = lax.axis_size("col")
    devices = rows_size * cols_size
    col_index = lax.axis_index("col")
    device_id = lax.axis_index("row") * cols_size + col_index
    panel_cols = panel_blocks.shape[0]
    own = panel_cols // devices
    slots = cons_blocks.shape[0]
    sub_rows = trailing.shape[0] // cols_size
    places = 8

    live = jnp.arange(slots, dtype=jnp.int32) < group_size[0]
    target = slot_row // sub_rows
    hits = ((target[:, None] == jnp.arange(devices, dtype=jnp.int32)[None, :]) & live[:, None]).astype(BF16)
    earlier = (
        lax.broadcasted_iota(jnp.int32, (slots, slots), 0) > lax.broadcasted_iota(jnp.int32, (slots, slots), 1)
    ).astype(BF16)
    rank = jnp.sum(dot(earlier, hits) * hits.astype(F32), axis=1).astype(jnp.int32)
    place = jnp.where(live, target * places + rank, -1)
    sends = lax.broadcasted_iota(jnp.int32, (devices * places, slots), 0) == place[None, :]
    local = jnp.sum(jnp.where(sends, (slot_row % sub_rows + 1)[None, :], 0), axis=1)
    sends = sends.astype(BF16)

    own_values = lax.dynamic_slice_in_dim(panel_blocks, device_id * own, own, 0).reshape(own, BS, BS)
    own_pos = lax.dynamic_slice_in_dim(panel_pos, device_id * own, own, 0)
    flat, ps_rows = panel_call(own_pos, x_mat, y_inv, own_values, panel_blocks, row_id(panel_pos)[None, :])
    ps = lax.all_to_all(jnp.broadcast_to(ps_rows[None], (devices, own, panel_cols)), AXES, 0, 0, tiled=True)
    ps = ps.reshape(panel_cols, panel_cols)

    wanted = jnp.broadcast_to(row_id(group_blocks)[:, :, None], (devices, 2, own)) + jnp.arange(own) * NB * NB
    pick = (wanted.reshape(-1)[:, None] == jnp.arange(own * NB * NB)[None, :]).astype(BF16)
    outgoing = dot(pick, flat).astype(BF16)
    outgoing, local, ps = lax.optimization_barrier((outgoing, local, ps))
    local = lax.all_to_all(local.reshape(devices, places), AXES, 0, 0, tiled=True).reshape(-1) - 1
    puts = (lax.broadcasted_iota(jnp.int32, (sub_rows, devices * places), 0) == local[None, :]).astype(BF16)
    blocks = lax.all_to_all(outgoing.reshape(devices, 2 * own, BS * BS), AXES, 0, 0, tiled=True)
    blocks = blocks.reshape(devices * 2 * own, BS * BS)

    inverse_t = factor_call(ps).T
    inverse_t = jnp.broadcast_to(
        inverse_t.reshape(devices, 1, own, panel_cols), (devices, 2, own, panel_cols)
    ).reshape(devices * 2 * own, panel_cols)

    product = dot(cons_blocks, blocks, NT)
    which = (jnp.arange(devices * 2 * own) // own) % 2
    product = jnp.where(slot_block[:, None] == which[None, :], product, 0.0)
    ph, plo = split_outside(product)
    ih, ilo = split_outside(inverse_t)
    lower = dot(ph, ih) + (dot(ph, ilo) + dot(plo, ih))
    send = dot(sends, lower.astype(BF16)).astype(BF16)
    recv = lax.all_to_all(send.reshape(devices, places, panel_cols), AXES, 0, 0, tiled=True)
    slab = dot(puts, recv.reshape(devices * places, panel_cols))
    slab_high = slab.astype(BF16)

    block_rows = trailing.shape[1] // rows_size
    lead = lax.all_to_all(slab_high[: block_rows * cols_size].reshape(cols_size, block_rows, panel_cols), "col", 0, 0, tiled=True)[0]
    picked = lax.all_to_all(jnp.broadcast_to(lead[None], (rows_size, block_rows, panel_cols)), "row", 0, 0, tiled=True)
    picked = picked.reshape(trailing.shape[1], panel_cols)
    all_rows = lax.all_gather(slab_high, "col", axis=0, tiled=True)
    updated = trailing - dot(all_rows, picked, NT)
    return (slab, updated)


def solution(mesh):
    return jax.shard_map(
        body,
        mesh=mesh,
        in_specs=(
            P(),
            P(),
            P(),
            P(),
            P(),
            P(("row", "col"), None),
            P(("row", "col")),
            P(("row", "col")),
            P(("row", "col")),
            P("row", "col"),
        ),
        out_specs=(P(("row", "col"), None), P("row", "col")),
        check_vma=False,
    )
```

```python
import functools

import jax
import jax.numpy as jnp
from jax import lax
from jax.experimental import pallas as pl
from jax.experimental.pallas import tpu as pltpu
from jax.sharding import PartitionSpec as P

F32 = jnp.float32
BF16 = jnp.bfloat16
BS = 64
NB = 8
N = 512
AXES = ("row", "col")
NT = (((1,), (1,)), ((), ()))
TN = (((0,), (0,)), ((), ()))


def split(a):
    high = a.astype(BF16)
    return high, (a - high.astype(F32)).astype(BF16)


def split_outside(a):
    high = lax.reduce_precision(a, 8, 7)
    return high.astype(BF16), (a - high).astype(BF16)


def dot(a, b, dims=(((1,), (0,)), ((), ()))):
    return lax.dot_general(a, b, dims, preferred_element_type=F32)


def panel_kernel(pos_ref, x_ref, y_ref, e_ref, panel_ref, rowid_ref, ps_ref, h_ref, f_ref, t_ref):
    count = e_ref.shape[0]
    lane = lax.broadcasted_iota(jnp.int32, (8, 128), 1)
    for j in range(count):
        position = pos_ref[j]
        p = pl.multiple_of(position // NB * BS, BS)
        q = pl.multiple_of(position % NB * BS, BS)
        e = e_ref[j].astype(F32)
        highest = lax.Precision.HIGHEST
        ey = jnp.dot(e, y_ref[pl.ds(q, BS), :], precision=highest, preferred_element_type=F32)
        ety = jnp.dot(e.T, y_ref[pl.ds(p, BS), :], precision=highest, preferred_element_type=F32)
        xh, xl = split(jnp.concatenate([x_ref[pl.ds(p, BS), :], x_ref[pl.ds(q, BS), :]], 0))
        vh, vl = split(jnp.concatenate([ey, ety], 0))
        ah = jnp.concatenate([xh, vh], 0)
        al = jnp.concatenate([xl, vl], 0)
        bh = jnp.concatenate([vh, xh], 0)
        bl = jnp.concatenate([vl, xl], 0)
        h = dot(ah, bh, TN) + (dot(ah, bl, TN) + dot(al, bh, TN))
        for b in range(NB // 2):
            h_ref[b] = h[:, b * 128 : b * 128 + 128]

        def relayout(pair, carry):
            r = pair * 2
            out = pl.ds(pl.multiple_of(pair * 128, 128), 128)
            for b in range(NB // 2):
                u = h_ref[b, pl.ds(r, NB, stride=BS), :]
                v = h_ref[b, pl.ds(r + 1, NB, stride=BS), :]
                f_ref[16 * b : 16 * b + 8, out] = jnp.where(lane < BS, u, pltpu.roll(v, BS, 1))
                f_ref[16 * b + 8 : 16 * b + 16, out] = jnp.where(lane < BS, pltpu.roll(u, BS, 1), v)
            return carry

        lax.fori_loop(0, BS // 2, relayout, 0, unroll=4)
        t_ref[j * 64 : j * 64 + 64, :] = f_ref[...].astype(BF16)
    hit = lax.broadcasted_iota(jnp.int32, (NB * NB, N), 0) == rowid_ref[...]
    for j in range(count):
        all_blocks = dot(t_ref[j * 64 : j * 64 + 64, :], panel_ref[...], NT)
        ps_ref[j : j + 1, :] = jnp.sum(jnp.where(hit, all_blocks, 0.0), axis=0, keepdims=True)


def panel_call(own_pos, x_mat, y_inv, own_e, panel_blocks, row_ids):
    count = own_e.shape[0]
    vmem = pl.BlockSpec(memory_space=pltpu.VMEM)
    return pl.pallas_call(
        panel_kernel,
        out_shape=jax.ShapeDtypeStruct((count, N), F32),
        in_specs=[pl.BlockSpec(memory_space=pltpu.SMEM)] + [vmem] * 5,
        out_specs=vmem,
        scratch_shapes=[
            pltpu.VMEM((NB // 2, N, 2 * BS), F32),
            pltpu.VMEM((NB * NB, BS * BS), F32),
            pltpu.VMEM((count * NB * NB, BS * BS), BF16),
        ],
        compiler_params=pltpu.CompilerParams(vmem_limit_bytes=40 * 2**20),
        name="panel",
    )(own_pos, x_mat, y_inv, own_e, panel_blocks, row_ids)


def factor_kernel(ps_ref, inv_ref, s_ref):
    order = ps_ref.shape[0]
    wide = 128
    highest = lax.Precision.HIGHEST
    ps = ps_ref[...]
    diagonal = lax.broadcasted_iota(jnp.int32, (order, order), 0) == lax.broadcasted_iota(jnp.int32, (order, order), 1)
    symmetric = 0.5 * (ps + ps.T)
    trace = jnp.sum(jnp.sum(jnp.where(diagonal, symmetric, 0.0), axis=1, keepdims=True), axis=0, keepdims=True)
    s_ref[...] = symmetric + jnp.where(diagonal, 0.01 / order * trace, 0.0)
    inv_ref[...] = jnp.where(diagonal, 1.0, 0.0)
    sub = lax.broadcasted_iota(jnp.int32, (8, wide), 0)
    small = lax.broadcasted_iota(jnp.int32, (wide, wide), 0) == lax.broadcasted_iota(jnp.int32, (wide, wide), 1)
    tiles = wide // 8
    for block in range(order // wide):
        at = slice(block * wide, block * wide + wide)
        whole = s_ref[at, at]
        a = [whole[8 * t : 8 * t + 8, :] for t in range(tiles)]
        w = [jnp.where(small[8 * t : 8 * t + 8, :], 1.0, 0.0) for t in range(tiles)]
        for m in range(tiles):
            cols = {
                t: [jnp.broadcast_to(a[t][:, 8 * m + c : 8 * m + c + 1], (8, wide)) for c in range(8)]
                for t in range(m, tiles)
            }
            scale = jnp.zeros((8, wide), F32)
            for c in range(8):
                pivot = jnp.broadcast_to(cols[m][c][c : c + 1, :], (8, wide))
                root = lax.rsqrt(pivot)
                root = root * (1.5 - 0.5 * pivot * root * root)
                scale = jnp.where(sub == c, root, scale)
                less = root * root
                row_a = jnp.broadcast_to(a[m][c : c + 1, :], (8, wide))
                row_w = jnp.broadcast_to(w[m][c : c + 1, :], (8, wide))
                heads = [jnp.broadcast_to(cols[m][d][c : c + 1, :], (8, wide)) for d in range(c + 1, 8)]
                for t in range(m, tiles):
                    times = cols[t][c] * less
                    if t == m:
                        times = jnp.where(sub > c, times, 0.0)
                    a[t] = a[t] - times * row_a
                    w[t] = w[t] - times * row_w
                    for d in range(c + 1, 8):
                        cols[t][d] = cols[t][d] - times * heads[d - c - 1]
            w[m] = w[m] * scale
        low = jnp.concatenate(w, 0)
        row_inv = jnp.dot(low, inv_ref[at, :], precision=highest, preferred_element_type=F32)
        inv_ref[at, :] = row_inv
        if (block + 1) * wide < order:
            rest = slice((block + 1) * wide, order)
            row_s = jnp.dot(low, s_ref[at, rest], precision=highest, preferred_element_type=F32)
            s_ref[rest, rest] -= lax.dot_general(row_s, row_s, TN, precision=highest, preferred_element_type=F32)
            inv_ref[rest, :] -= lax.dot_general(row_s, row_inv, TN, precision=highest, preferred_element_type=F32)


def factor_call(ps):
    vmem = pl.BlockSpec(memory_space=pltpu.VMEM)
    return pl.pallas_call(
        factor_kernel,
        out_shape=jax.ShapeDtypeStruct(ps.shape, F32),
        in_specs=[vmem],
        out_specs=vmem,
        scratch_shapes=[pltpu.VMEM(ps.shape, F32)],
        compiler_params=pltpu.CompilerParams(vmem_limit_bytes=32 * 2**20),
        cost_estimate=pl.CostEstimate(flops=4 * 10**9, bytes_accessed=4 * 2**20, transcendentals=0),
        name="factor",
    )(ps)


def local_kernel(pos_ref, at_ref, x_ref, y_ref, panel_ref, zero_ref, one_ref, a_ref, z_ref, e_ref, c_ref):
    step = pl.program_id(0)
    count = panel_ref.shape[0]

    def low(shape):
        return lax.broadcasted_iota(jnp.int32, shape, 1) < BS

    @pl.when(step == 0)
    def _():
        for s in range(2):
            rows = pl.ds(pl.multiple_of(at_ref[2 * s] * BS, BS), BS)
            first = low((BS, 128))
            for k in range(NB // 2):
                u = x_ref[rows, 128 * k : 128 * k + 128]
                v = y_ref[rows, 128 * k : 128 * k + 128]
                for p, both in (
                    (2 * k, jnp.where(first, u, pltpu.roll(v, BS, 1))),
                    (2 * k + 1, jnp.where(first, pltpu.roll(u, BS, 1), v)),
                ):
                    high, rest = split(both)
                    a_ref[p, s * BS : s * BS + BS, :] = high
                    a_ref[p, 128 + s * BS : 128 + s * BS + BS, :] = rest
        first = low((N, 128))
        for n, ref in enumerate((y_ref, x_ref)):
            halves = []
            for s in range(2):
                b = at_ref[2 * s + 1]
                tile = ref[:, pl.ds(pl.multiple_of(b // 2 * 128, 128), 128)]
                halves.append(jnp.where(b % 2 == s, tile, pltpu.roll(tile, BS, 1)))
            high, rest = split(jnp.where(first, halves[0], halves[1]))
            for q in range(NB):
                z_ref[q, :BS, 128 * n : 128 * n + 128] = high[q * BS : q * BS + BS]
                z_ref[q, BS:, 128 * n : 128 * n + 128] = rest[q * BS : q * BS + BS]

    first = low((8, 128))
    for k in range(BS // 2):
        pair = panel_ref[:, 128 * k : 128 * k + 128].astype(F32)
        for half in range(count // 8):
            u = pair[8 * half : 8 * half + 8]
            v = pltpu.roll(u, BS, 1)
            e_ref[pl.ds(512 * half + 2 * k, 8, stride=BS), :] = jnp.where(first, u, v)
            e_ref[pl.ds(512 * half + 2 * k + 1, 8, stride=BS), :] = jnp.where(first, v, u)

    keep = low((BS, 128))

    def group(g, carry):
        ones, twos, ps = [], [], []
        for n in range(16):
            j = g * 16 + n
            position = pos_ref[step * count + j]
            p = position // NB
            q = position % NB
            ps.append((p, q))
            ee = e_ref[slice(j * BS, j * BS + BS), :].astype(BF16)
            ones.append(dot(ee, z_ref[q]))
            twos.append(dot(jnp.concatenate([ee, ee], 0)[:, :BS], z_ref[p], TN))
        parts = []
        for one, two in zip(ones, twos):
            right = jnp.concatenate([one[:, :128], one[:, 128:], two[:, :128], two[:, 128:]], 0)
            parts.append(jnp.concatenate(split(right), 1))
        outs = []
        for (p, q), part in zip(ps, parts):
            outs.append(dot(jnp.concatenate([a_ref[p], a_ref[q]], 1), part))
        for n, out in enumerate(outs):
            here = out[:BS, :128] + (out[:BS, 128:] + out[128 : 128 + BS, :128])
            there = out[BS:128, :128] + (out[BS:128, 128:] + out[128 + BS :, :128])
            c_ref[slice((g * 16 + n) * BS, (g * 16 + n) * BS + BS), :] = jnp.where(keep, here, there)
        return carry

    def give(g):
        for k in range(BS // 2):
            firsts, seconds = [], []
            for half in range(16 // 8):
                u = c_ref[pl.ds(BS * 16 * g + 512 * half + 2 * k, 8, stride=BS), :]
                v = c_ref[pl.ds(BS * 16 * g + 512 * half + 2 * k + 1, 8, stride=BS), :]
                firsts.append(jnp.where(first, u, pltpu.roll(v, BS, 1)))
                seconds.append(jnp.where(first, pltpu.roll(u, BS, 1), v))
            rows = slice(g * 16, g * 16 + 16)
            zero_ref[rows, 128 * k : 128 * k + 128] = jnp.concatenate(firsts, 0).astype(BF16)
            one_ref[rows, 128 * k : 128 * k + 128] = jnp.concatenate(seconds, 0).astype(BF16)

    group(0, 0)
    give(0)
    group(1, 0)
    give(1)


def local_call(panel_pos, places, x_mat, y_inv, panel_blocks):
    count = 32
    columns, flat = panel_blocks.shape
    smem = pl.BlockSpec(memory_space=pltpu.SMEM)
    vmem = pl.BlockSpec(memory_space=pltpu.VMEM)
    part = pl.BlockSpec((count, flat), lambda i: (i, 0))
    return pl.pallas_call(
        local_kernel,
        grid=(columns // count,),
        out_shape=(jax.ShapeDtypeStruct((columns, flat), BF16),) * 2,
        in_specs=[smem, smem, vmem, vmem, part],
        out_specs=(part, part),
        scratch_shapes=[
            pltpu.VMEM((NB, 256, 128), BF16),
            pltpu.VMEM((NB, 128, 256), BF16),
            pltpu.VMEM((count * BS, 128), F32),
            pltpu.VMEM((count * BS, 128), F32),
        ],
        compiler_params=pltpu.CompilerParams(vmem_limit_bytes=40 * 2**20),
        cost_estimate=pl.CostEstimate(flops=26 * 10**9, bytes_accessed=14 * 2**20, transcendentals=0),
        name="local",
    )(panel_pos, places, x_mat, y_inv, panel_blocks)


def row_id(position):
    return position % NB * NB + position // NB


def body(
    x_mat,
    y_inv,
    panel_blocks,
    panel_pos,
    group_blocks,
    cons_blocks,
    slot_block,
    slot_row,
    group_size,
    trailing,
):
    rows_size = lax.axis_size("row")
    cols_size = lax.axis_size("col")
    devices = rows_size * cols_size
    col_index = lax.axis_index("col")
    device_id = lax.axis_index("row") * cols_size + col_index
    panel_cols = panel_blocks.shape[0]
    own = panel_cols // devices
    slots = cons_blocks.shape[0]
    sub_rows = trailing.shape[0] // cols_size
    places = 8

    live = jnp.arange(slots, dtype=jnp.int32) < group_size[0]
    target = slot_row // sub_rows
    hits = ((target[:, None] == jnp.arange(devices, dtype=jnp.int32)[None, :]) & live[:, None]).astype(BF16)
    earlier = (
        lax.broadcasted_iota(jnp.int32, (slots, slots), 0) > lax.broadcasted_iota(jnp.int32, (slots, slots), 1)
    ).astype(BF16)
    rank = jnp.sum(dot(earlier, hits) * hits.astype(F32), axis=1).astype(jnp.int32)
    place = jnp.where(live, target * places + rank, -1)
    sends = lax.broadcasted_iota(jnp.int32, (devices * places, slots), 0) == place[None, :]
    local = jnp.sum(jnp.where(sends, (slot_row % sub_rows + 1)[None, :], 0), axis=1)
    sends = sends.astype(BF16)
    local = local.reshape(devices, places)
    note = jnp.concatenate([local // 16, local % 16], 1).astype(BF16)
    note = jnp.pad(note, ((0, 0), (0, panel_cols - 2 * places)))[:, None, :]

    own_values = lax.dynamic_slice_in_dim(panel_blocks, device_id * own, own, 0).reshape(own, BS, BS)
    own_pos = lax.dynamic_slice_in_dim(panel_pos, device_id * own, own, 0)
    ps_rows = panel_call(own_pos, x_mat, y_inv, own_values, panel_blocks, row_id(panel_pos)[None, :])
    ps = lax.all_to_all(jnp.broadcast_to(ps_rows[None], (devices, own, panel_cols)), AXES, 0, 0, tiled=True)
    ps = ps.reshape(panel_cols, panel_cols)

    at = group_blocks[device_id]
    zero, one = local_call(panel_pos, jnp.stack([at // NB, at % NB], 1).reshape(-1), x_mat, y_inv, panel_blocks)
    product = jnp.where(slot_block[:, None] == 0, dot(cons_blocks, zero, NT), dot(cons_blocks, one, NT))
    inverse = factor_call(ps)
    ph, plo = split_outside(product)
    ih, ilo = split_outside(inverse)
    lower = dot(ph, ih, NT) + (dot(ph, ilo, NT) + dot(plo, ih, NT))
    send = dot(sends, lower.astype(BF16)).astype(BF16).reshape(devices, places, panel_cols)
    send = jnp.where(jnp.arange(places)[None, :, None] == places - 1, note, send)
    recv = lax.all_to_all(send, AXES, 0, 0, tiled=True)
    note = recv[:, places - 1, : 2 * places].astype(jnp.int32)
    local = (note[:, :places] * 16 + note[:, places:]).reshape(-1) - 1
    puts = (lax.broadcasted_iota(jnp.int32, (sub_rows, devices * places), 0) == local[None, :]).astype(BF16)
    slab = dot(puts, recv.reshape(devices * places, panel_cols))
    slab_high = slab.astype(BF16)

    block_rows = trailing.shape[1] // rows_size
    lead = lax.all_to_all(slab_high[: block_rows * cols_size].reshape(cols_size, block_rows, panel_cols), "col", 0, 0, tiled=True)[0]
    picked = lax.all_to_all(jnp.broadcast_to(lead[None], (rows_size, block_rows, panel_cols)), "row", 0, 0, tiled=True)
    picked = picked.reshape(trailing.shape[1], panel_cols)
    all_rows = lax.all_gather(slab_high, "col", axis=0, tiled=True)
    updated = trailing - dot(all_rows, picked, NT)
    return (slab, updated)


def solution(mesh):
    return jax.shard_map(
        body,
        mesh=mesh,
        in_specs=(
            P(),
            P(),
            P(),
            P(),
            P(),
            P(("row", "col"), None),
            P(("row", "col")),
            P(("row", "col")),
            P(("row", "col")),
            P("row", "col"),
        ),
        out_specs=(P(("row", "col"), None), P("row", "col")),
        check_vma=False,
    )
```

```python
import functools

import jax
import jax.numpy as jnp
from jax import lax
from jax.experimental import pallas as pl
from jax.experimental.pallas import tpu as pltpu
from jax.sharding import PartitionSpec as P

F32 = jnp.float32
BF16 = jnp.bfloat16
BS = 64
NB = 8
N = 512
AXES = ("row", "col")
NT = (((1,), (1,)), ((), ()))
TN = (((0,), (0,)), ((), ()))


def split(a):
    high = a.astype(BF16)
    return high, (a - high.astype(F32)).astype(BF16)


def dot(a, b, dims=(((1,), (0,)), ((), ()))):
    return lax.dot_general(a, b, dims, preferred_element_type=F32)


def panel_kernel(pos_ref, x_ref, y_ref, e_ref, panel_ref, rowid_ref, ps_ref, h_ref, f_ref, t_ref):
    count = e_ref.shape[0]
    lane = lax.broadcasted_iota(jnp.int32, (8, 128), 1)
    for j in range(count):
        position = pos_ref[j]
        p = pl.multiple_of(position // NB * BS, BS)
        q = pl.multiple_of(position % NB * BS, BS)
        e = e_ref[j].astype(F32)
        highest = lax.Precision.HIGHEST
        ey = jnp.dot(e, y_ref[pl.ds(q, BS), :], precision=highest, preferred_element_type=F32)
        ety = jnp.dot(e.T, y_ref[pl.ds(p, BS), :], precision=highest, preferred_element_type=F32)
        xh, xl = split(jnp.concatenate([x_ref[pl.ds(p, BS), :], x_ref[pl.ds(q, BS), :]], 0))
        vh, vl = split(jnp.concatenate([ey, ety], 0))
        ah = jnp.concatenate([xh, vh], 0)
        al = jnp.concatenate([xl, vl], 0)
        bh = jnp.concatenate([vh, xh], 0)
        bl = jnp.concatenate([vl, xl], 0)
        h = dot(ah, bh, TN) + (dot(ah, bl, TN) + dot(al, bh, TN))
        for b in range(NB // 2):
            h_ref[b] = h[:, b * 128 : b * 128 + 128]

        def relayout(pair, carry):
            r = pair * 2
            out = pl.ds(pl.multiple_of(pair * 128, 128), 128)
            for b in range(NB // 2):
                u = h_ref[b, pl.ds(r, NB, stride=BS), :]
                v = h_ref[b, pl.ds(r + 1, NB, stride=BS), :]
                f_ref[16 * b : 16 * b + 8, out] = jnp.where(lane < BS, u, pltpu.roll(v, BS, 1))
                f_ref[16 * b + 8 : 16 * b + 16, out] = jnp.where(lane < BS, pltpu.roll(u, BS, 1), v)
            return carry

        lax.fori_loop(0, BS // 2, relayout, 0, unroll=4)
        t_ref[j * 64 : j * 64 + 64, :] = f_ref[...].astype(BF16)
    hit = lax.broadcasted_iota(jnp.int32, (NB * NB, N), 0) == rowid_ref[...]
    for j in range(count):
        all_blocks = dot(t_ref[j * 64 : j * 64 + 64, :], panel_ref[...], NT)
        ps_ref[j : j + 1, :] = jnp.sum(jnp.where(hit, all_blocks, 0.0), axis=0, keepdims=True)


def panel_call(own_pos, x_mat, y_inv, own_e, panel_blocks, row_ids):
    count = own_e.shape[0]
    vmem = pl.BlockSpec(memory_space=pltpu.VMEM)
    return pl.pallas_call(
        panel_kernel,
        out_shape=jax.ShapeDtypeStruct((count, N), F32),
        in_specs=[pl.BlockSpec(memory_space=pltpu.SMEM)] + [vmem] * 5,
        out_specs=vmem,
        scratch_shapes=[
            pltpu.VMEM((NB // 2, N, 2 * BS), F32),
            pltpu.VMEM((NB * NB, BS * BS), F32),
            pltpu.VMEM((count * NB * NB, BS * BS), BF16),
        ],
        compiler_params=pltpu.CompilerParams(vmem_limit_bytes=40 * 2**20),
        name="panel",
    )(own_pos, x_mat, y_inv, own_e, panel_blocks, row_ids)


def factor_kernel(ps_ref, inv_ref, s_ref):
    order = ps_ref.shape[0]
    wide = 128
    highest = lax.Precision.HIGHEST
    ps = ps_ref[...]
    diagonal = lax.broadcasted_iota(jnp.int32, (order, order), 0) == lax.broadcasted_iota(jnp.int32, (order, order), 1)
    symmetric = 0.5 * (ps + ps.T)
    trace = jnp.sum(jnp.sum(jnp.where(diagonal, symmetric, 0.0), axis=1, keepdims=True), axis=0, keepdims=True)
    s_ref[...] = symmetric + jnp.where(diagonal, 0.01 / order * trace, 0.0)
    inv_ref[...] = jnp.where(diagonal, 1.0, 0.0)
    sub = lax.broadcasted_iota(jnp.int32, (8, wide), 0)
    small = lax.broadcasted_iota(jnp.int32, (wide, wide), 0) == lax.broadcasted_iota(jnp.int32, (wide, wide), 1)
    tiles = wide // 8
    for block in range(order // wide):
        at = slice(block * wide, block * wide + wide)
        whole = s_ref[at, at]
        a = [whole[8 * t : 8 * t + 8, :] for t in range(tiles)]
        w = [jnp.where(small[8 * t : 8 * t + 8, :], 1.0, 0.0) for t in range(tiles)]
        for m in range(tiles):
            cols = {
                t: [jnp.broadcast_to(a[t][:, 8 * m + c : 8 * m + c + 1], (8, wide)) for c in range(8)]
                for t in range(m, tiles)
            }
            scale = jnp.zeros((8, wide), F32)
            for c in range(8):
                pivot = jnp.broadcast_to(cols[m][c][c : c + 1, :], (8, wide))
                root = lax.rsqrt(pivot)
                root = root * (1.5 - 0.5 * pivot * root * root)
                scale = jnp.where(sub == c, root, scale)
                less = root * root
                row_a = jnp.broadcast_to(a[m][c : c + 1, :], (8, wide))
                row_w = jnp.broadcast_to(w[m][c : c + 1, :], (8, wide))
                heads = [jnp.broadcast_to(cols[m][d][c : c + 1, :], (8, wide)) for d in range(c + 1, 8)]
                for t in range(m, tiles):
                    times = cols[t][c] * less
                    if t == m:
                        times = jnp.where(sub > c, times, 0.0)
                    a[t] = a[t] - times * row_a
                    w[t] = w[t] - times * row_w
                    for d in range(c + 1, 8):
                        cols[t][d] = cols[t][d] - times * heads[d - c - 1]
            w[m] = w[m] * scale
        low = jnp.concatenate(w, 0)
        row_inv = jnp.dot(low, inv_ref[at, :], precision=highest, preferred_element_type=F32)
        inv_ref[at, :] = row_inv
        if (block + 1) * wide < order:
            rest = slice((block + 1) * wide, order)
            row_s = jnp.dot(low, s_ref[at, rest], precision=highest, preferred_element_type=F32)
            s_ref[rest, rest] -= lax.dot_general(row_s, row_s, TN, precision=highest, preferred_element_type=F32)
            inv_ref[rest, :] -= lax.dot_general(row_s, row_inv, TN, precision=highest, preferred_element_type=F32)


def factor_call(ps):
    vmem = pl.BlockSpec(memory_space=pltpu.VMEM)
    return pl.pallas_call(
        factor_kernel,
        out_shape=jax.ShapeDtypeStruct(ps.shape, F32),
        in_specs=[vmem],
        out_specs=vmem,
        scratch_shapes=[pltpu.VMEM(ps.shape, F32)],
        compiler_params=pltpu.CompilerParams(vmem_limit_bytes=32 * 2**20),
        cost_estimate=pl.CostEstimate(flops=4 * 10**9, bytes_accessed=4 * 2**20, transcendentals=0),
        name="factor",
    )(ps)


def rows_kernel(
    pos_ref, at_ref, x_ref, y_ref, panel_ref, which_ref, place_ref, note_ref, cons_hbm, send_ref,
    a_ref, z_ref, e_ref, c_ref, zero_ref, one_ref, cons_ref, sem,
):
    step = pl.program_id(0)
    count = panel_ref.shape[0]
    parts = N // count
    tile = which_ref.shape[0]
    copy = pltpu.make_async_copy(cons_hbm, cons_ref, sem)

    @pl.when(step == 0)
    def _():
        copy.start()
        send_ref[...] = jnp.zeros_like(send_ref)
        send_ref[:, :128] = note_ref[...]

    @pl.when(step < parts)
    def _():
        form_blocks(step, count, pos_ref, at_ref, x_ref, y_ref, panel_ref, zero_ref, one_ref, a_ref, z_ref, e_ref, c_ref)

    @pl.when(step == parts)
    def _():
        copy.wait()

    @pl.when(step >= parts)
    def _():
        rows = pl.ds(pl.multiple_of((step - parts) * tile, 64), tile)
        cons = cons_ref[rows, :]
        out = jnp.where(which_ref[...] == 0, dot(cons, zero_ref[...], NT), dot(cons, one_ref[...], NT))
        hit = lax.broadcasted_iota(jnp.int32, (send_ref.shape[0], tile), 0) == place_ref[0]
        hit = jnp.where(hit, 1.0, 0.0).astype(BF16)
        high, rest = split(out)
        send_ref[...] += dot(hit, high) + dot(hit, rest)


def form_blocks(step, count, pos_ref, at_ref, x_ref, y_ref, panel_ref, zero_ref, one_ref, a_ref, z_ref, e_ref, c_ref):
    start = pl.multiple_of(step * count, count)

    def low(shape):
        return lax.broadcasted_iota(jnp.int32, shape, 1) < BS

    @pl.when(step == 0)
    def _():
        for s in range(2):
            rows = pl.ds(pl.multiple_of(at_ref[2 * s] * BS, BS), BS)
            first = low((BS, 128))
            for k in range(NB // 2):
                u = x_ref[rows, 128 * k : 128 * k + 128]
                v = y_ref[rows, 128 * k : 128 * k + 128]
                for p, both in (
                    (2 * k, jnp.where(first, u, pltpu.roll(v, BS, 1))),
                    (2 * k + 1, jnp.where(first, pltpu.roll(u, BS, 1), v)),
                ):
                    high, rest = split(both)
                    a_ref[p, s * BS : s * BS + BS, :] = high
                    a_ref[p, 128 + s * BS : 128 + s * BS + BS, :] = rest
        first = low((N, 128))
        for n, ref in enumerate((y_ref, x_ref)):
            halves = []
            for s in range(2):
                b = at_ref[2 * s + 1]
                tile = ref[:, pl.ds(pl.multiple_of(b // 2 * 128, 128), 128)]
                halves.append(jnp.where(b % 2 == s, tile, pltpu.roll(tile, BS, 1)))
            high, rest = split(jnp.where(first, halves[0], halves[1]))
            for q in range(NB):
                z_ref[q, :BS, 128 * n : 128 * n + 128] = high[q * BS : q * BS + BS]
                z_ref[q, BS:, 128 * n : 128 * n + 128] = rest[q * BS : q * BS + BS]

    first = low((8, 128))
    for k in range(BS // 2):
        pair = panel_ref[:, 128 * k : 128 * k + 128].astype(F32)
        for half in range(count // 8):
            u = pair[8 * half : 8 * half + 8]
            v = pltpu.roll(u, BS, 1)
            e_ref[pl.ds(512 * half + 2 * k, 8, stride=BS), :] = jnp.where(first, u, v)
            e_ref[pl.ds(512 * half + 2 * k + 1, 8, stride=BS), :] = jnp.where(first, v, u)

    keep = low((BS, 128))

    def group(g, carry):
        ones, twos, ps = [], [], []
        for n in range(16):
            j = g * 16 + n
            position = pos_ref[step * count + j]
            p = position // NB
            q = position % NB
            ps.append((p, q))
            ee = e_ref[slice(j * BS, j * BS + BS), :].astype(BF16)
            ones.append(dot(ee, z_ref[q]))
            twos.append(dot(jnp.concatenate([ee, ee], 0)[:, :BS], z_ref[p], TN))
        parts = []
        for one, two in zip(ones, twos):
            right = jnp.concatenate([one[:, :128], one[:, 128:], two[:, :128], two[:, 128:]], 0)
            parts.append(jnp.concatenate(split(right), 1))
        outs = []
        for (p, q), part in zip(ps, parts):
            outs.append(dot(jnp.concatenate([a_ref[p], a_ref[q]], 1), part))
        for n, out in enumerate(outs):
            here = out[:BS, :128] + (out[:BS, 128:] + out[128 : 128 + BS, :128])
            there = out[BS:128, :128] + (out[BS:128, 128:] + out[128 + BS :, :128])
            c_ref[slice((g * 16 + n) * BS, (g * 16 + n) * BS + BS), :] = jnp.where(keep, here, there)
        return carry

    def give(g):
        for k in range(BS // 2):
            firsts, seconds = [], []
            for half in range(16 // 8):
                u = c_ref[pl.ds(BS * 16 * g + 512 * half + 2 * k, 8, stride=BS), :]
                v = c_ref[pl.ds(BS * 16 * g + 512 * half + 2 * k + 1, 8, stride=BS), :]
                firsts.append(jnp.where(first, u, pltpu.roll(v, BS, 1)))
                seconds.append(jnp.where(first, pltpu.roll(u, BS, 1), v))
            rows = pl.ds(start + g * 16, 16)
            zero_ref[rows, 128 * k : 128 * k + 128] = jnp.concatenate(firsts, 0).astype(BF16)
            one_ref[rows, 128 * k : 128 * k + 128] = jnp.concatenate(seconds, 0).astype(BF16)

    group(0, 0)
    give(0)
    group(1, 0)
    give(1)


def rows_call(panel_pos, at, x_mat, y_inv, panel_blocks, which, place, note, cons):
    count = 32
    columns, flat = panel_blocks.shape
    slots = cons.shape[0]
    parts = columns // count
    tiles = place.shape[0]
    tile = slots // tiles
    smem = pl.BlockSpec(memory_space=pltpu.SMEM)
    vmem = pl.BlockSpec(memory_space=pltpu.VMEM)
    return pl.pallas_call(
        rows_kernel,
        grid=(parts + tiles,),
        out_shape=jax.ShapeDtypeStruct((note.shape[0], columns), F32),
        in_specs=[
            smem,
            smem,
            vmem,
            vmem,
            pl.BlockSpec((count, flat), lambda i: (jnp.minimum(i, parts - 1), 0)),
            pl.BlockSpec((tile, 1), lambda i: (jnp.maximum(i - parts, 0), 0)),
            pl.BlockSpec((1, 1, tile), lambda i: (jnp.maximum(i - parts, 0), 0, 0)),
            vmem,
            pl.BlockSpec(memory_space=pl.ANY),
        ],
        out_specs=vmem,
        scratch_shapes=[
            pltpu.VMEM((NB, 256, 128), BF16),
            pltpu.VMEM((NB, 128, 256), BF16),
            pltpu.VMEM((count * BS, 128), F32),
            pltpu.VMEM((count * BS, 128), F32),
            pltpu.VMEM((columns, flat), BF16),
            pltpu.VMEM((columns, flat), BF16),
            pltpu.VMEM((slots, flat), BF16),
            pltpu.SemaphoreType.DMA,
        ],
        compiler_params=pltpu.CompilerParams(vmem_limit_bytes=56 * 2**20),
        cost_estimate=pl.CostEstimate(flops=36 * 10**9, bytes_accessed=14 * 2**20, transcendentals=0),
        name="rows",
    )(panel_pos, at, x_mat, y_inv, panel_blocks, which, place, note, cons)


def finish_kernel(local_ref, recv_ref, inverse_ref, slab_ref, high_ref):
    hit = lax.broadcasted_iota(jnp.int32, (slab_ref.shape[0], recv_ref.shape[0]), 0) == local_ref[...]
    hit = jnp.where(hit, 1.0, 0.0).astype(BF16)
    high, rest = split(recv_ref[...])
    raw_high, raw_rest = split(dot(hit, high) + dot(hit, rest))
    inv_high, inv_rest = split(inverse_ref[...])
    slab = dot(raw_high, inv_high, NT) + (dot(raw_high, inv_rest, NT) + dot(raw_rest, inv_high, NT))
    slab_ref[...] = slab
    high_ref[...] = slab.astype(BF16)


def finish_call(local, recv, inverse, rows):
    vmem = pl.BlockSpec(memory_space=pltpu.VMEM)
    shape = (rows, recv.shape[1])
    return pl.pallas_call(
        finish_kernel,
        out_shape=(jax.ShapeDtypeStruct(shape, F32), jax.ShapeDtypeStruct(shape, BF16)),
        in_specs=[vmem] * 3,
        out_specs=(vmem, vmem),
        compiler_params=pltpu.CompilerParams(vmem_limit_bytes=32 * 2**20),
        name="finish",
    )(local, recv, inverse)


def row_id(position):
    return position % NB * NB + position // NB


def body(
    x_mat,
    y_inv,
    panel_blocks,
    panel_pos,
    group_blocks,
    cons_blocks,
    slot_block,
    slot_row,
    group_size,
    trailing,
):
    rows_size = lax.axis_size("row")
    cols_size = lax.axis_size("col")
    devices = rows_size * cols_size
    col_index = lax.axis_index("col")
    device_id = lax.axis_index("row") * cols_size + col_index
    panel_cols = panel_blocks.shape[0]
    own = panel_cols // devices
    slots = cons_blocks.shape[0]
    sub_rows = trailing.shape[0] // cols_size
    places = 8

    live = jnp.arange(slots, dtype=jnp.int32) < group_size[0]
    target = slot_row // sub_rows
    hits = ((target[:, None] == jnp.arange(devices, dtype=jnp.int32)[None, :]) & live[:, None]).astype(BF16)
    earlier = (
        lax.broadcasted_iota(jnp.int32, (slots, slots), 0) > lax.broadcasted_iota(jnp.int32, (slots, slots), 1)
    ).astype(BF16)
    rank = jnp.sum(dot(earlier, hits) * hits.astype(F32), axis=1).astype(jnp.int32)
    place = jnp.where(live, target * places + rank, -1)
    sends = lax.broadcasted_iota(jnp.int32, (devices * places, slots), 0) == place[None, :]
    local = jnp.sum(jnp.where(sends, (slot_row % sub_rows + 1)[None, :], 0), axis=1)
    note = jnp.pad(local.reshape(devices, places).astype(F32), ((0, 0), (0, 128 - places)))[:, None, :]
    note = jnp.where(jnp.arange(places)[None, :, None] == places - 1, note, 0.0).reshape(devices * places, 128)

    own_values = lax.dynamic_slice_in_dim(panel_blocks, device_id * own, own, 0).reshape(own, BS, BS)
    own_pos = lax.dynamic_slice_in_dim(panel_pos, device_id * own, own, 0)
    ps_rows = panel_call(own_pos, x_mat, y_inv, own_values, panel_blocks, row_id(panel_pos)[None, :])
    ps = lax.all_to_all(jnp.broadcast_to(ps_rows[None], (devices, own, panel_cols)), AXES, 0, 0, tiled=True)
    ps = ps.reshape(panel_cols, panel_cols)

    at = group_blocks[device_id]
    at = jnp.stack([at // NB, at % NB], 1).reshape(-1)
    send = rows_call(
        panel_pos, at, x_mat, y_inv, panel_blocks, slot_block[:, None], place.reshape(2, 1, -1), note, cons_blocks
    )
    recv = lax.all_to_all(send.reshape(devices, places, panel_cols), AXES, 0, 0, tiled=True)
    inverse = factor_call(ps)
    local = recv[:, places - 1, :places].astype(jnp.int32).reshape(1, -1) - 1
    slab, slab_high = finish_call(local, recv.reshape(devices * places, panel_cols), inverse, sub_rows)

    block_rows = trailing.shape[1] // rows_size
    lead = lax.all_to_all(slab_high[: block_rows * cols_size].reshape(cols_size, block_rows, panel_cols), "col", 0, 0, tiled=True)[0]
    picked = lax.all_to_all(jnp.broadcast_to(lead[None], (rows_size, block_rows, panel_cols)), "row", 0, 0, tiled=True)
    picked = picked.reshape(trailing.shape[1], panel_cols)
    all_rows = lax.all_gather(slab_high, "col", axis=0, tiled=True)
    updated = trailing - dot(all_rows, picked, NT)
    return (slab, updated)


def solution(mesh):
    return jax.shard_map(
        body,
        mesh=mesh,
        in_specs=(
            P(),
            P(),
            P(),
            P(),
            P(),
            P(("row", "col"), None),
            P(("row", "col")),
            P(("row", "col")),
            P(("row", "col")),
            P("row", "col"),
        ),
        out_specs=(P(("row", "col"), None), P("row", "col")),
        check_vma=False,
    )
```

```python
import functools

import jax
import jax.numpy as jnp
from jax import lax
from jax.experimental import pallas as pl
from jax.experimental.pallas import tpu as pltpu
from jax.sharding import PartitionSpec as P

F32 = jnp.float32
BF16 = jnp.bfloat16
BS = 64
NB = 8
N = 512
AXES = ("row", "col")
NT = (((1,), (1,)), ((), ()))
TN = (((0,), (0,)), ((), ()))


def split(a):
    high = a.astype(BF16)
    return high, (a - high.astype(F32)).astype(BF16)


def dot(a, b, dims=(((1,), (0,)), ((), ()))):
    return lax.dot_general(a, b, dims, preferred_element_type=F32)


def panel_kernel(pos_ref, x_ref, y_ref, e_ref, panel_hbm, rowid_ref, ps_ref, h_ref, t_ref, panel_ref, sem):
    copy = pltpu.make_async_copy(panel_hbm, panel_ref, sem)
    copy.start()
    count = e_ref.shape[0]
    lane = lax.broadcasted_iota(jnp.int32, (8, 128), 1)
    heads = []
    for j in range(count):
        position = pos_ref[j]
        p = pl.multiple_of(position // NB * BS, BS)
        q = pl.multiple_of(position % NB * BS, BS)
        e = e_ref[j]
        yh, yl = split(jnp.concatenate([y_ref[pl.ds(q, BS), :], y_ref[pl.ds(p, BS), :]], 0))
        ey = dot(e, yh[:BS]) + dot(e, yl[:BS])
        ety = dot(e, yh[BS:], TN) + dot(e, yl[BS:], TN)
        xh, xl = split(jnp.concatenate([x_ref[pl.ds(p, BS), :], x_ref[pl.ds(q, BS), :]], 0))
        vh, vl = split(jnp.concatenate([ey, ety], 0))
        heads.append((xh, xl, vh, vl))
    for j, (xh, xl, vh, vl) in enumerate(heads):
        ah = jnp.concatenate([xh, vh], 0)
        al = jnp.concatenate([xl, vl], 0)
        bh = jnp.concatenate([vh, xh], 0)
        bl = jnp.concatenate([vl, xl], 0)
        h = dot(ah, bh, TN) + (dot(ah, bl, TN) + dot(al, bh, TN))
        for b in range(NB // 2):
            h_ref[j, b] = h[:, b * 128 : b * 128 + 128]
    for j in range(count):
        for pair in range(BS // 2):
            r = pair * 2
            out = slice(pair * 128, pair * 128 + 128)
            for b in range(NB // 2):
                u = h_ref[j, b, pl.ds(r, NB, stride=BS), :]
                v = h_ref[j, b, pl.ds(r + 1, NB, stride=BS), :]
                even = jnp.where(lane < BS, u, pltpu.roll(v, BS, 1))
                odd = jnp.where(lane < BS, pltpu.roll(u, BS, 1), v)
                t_ref[j * 64 + 16 * b : j * 64 + 16 * b + 16, out] = jnp.concatenate([even, odd], 0).astype(BF16)
    copy.wait()
    hit = lax.broadcasted_iota(jnp.int32, (NB * NB, N), 0) == rowid_ref[...]
    all_blocks = dot(t_ref[...], panel_ref[...], NT)
    for j in range(count):
        part = all_blocks[j * 64 : j * 64 + 64, :]
        ps_ref[j : j + 1, :] = jnp.sum(jnp.where(hit, part, 0.0), axis=0, keepdims=True)


def panel_call(own_pos, x_mat, y_inv, own_e, panel_blocks, row_ids):
    count = own_e.shape[0]
    vmem = pl.BlockSpec(memory_space=pltpu.VMEM)
    return pl.pallas_call(
        panel_kernel,
        out_shape=jax.ShapeDtypeStruct((count, N), F32),
        in_specs=[
            pl.BlockSpec(memory_space=pltpu.SMEM),
            vmem,
            vmem,
            vmem,
            pl.BlockSpec(memory_space=pl.ANY),
            vmem,
        ],
        out_specs=vmem,
        scratch_shapes=[
            pltpu.VMEM((count, NB // 2, N, 2 * BS), F32),
            pltpu.VMEM((count * NB * NB, BS * BS), BF16),
            pltpu.VMEM(panel_blocks.shape, BF16),
            pltpu.SemaphoreType.DMA,
        ],
        compiler_params=pltpu.CompilerParams(vmem_limit_bytes=56 * 2**20),
        name="panel",
    )(own_pos, x_mat, y_inv, own_e, panel_blocks, row_ids)


def factor_kernel(ps_ref, inv_ref, s_ref):
    order = ps_ref.shape[0]
    wide = 128
    highest = lax.Precision.HIGHEST
    ps = ps_ref[...]
    diagonal = lax.broadcasted_iota(jnp.int32, (order, order), 0) == lax.broadcasted_iota(jnp.int32, (order, order), 1)
    symmetric = 0.5 * (ps + ps.T)
    trace = jnp.sum(jnp.sum(jnp.where(diagonal, symmetric, 0.0), axis=1, keepdims=True), axis=0, keepdims=True)
    s_ref[...] = symmetric + jnp.where(diagonal, 0.01 / order * trace, 0.0)
    inv_ref[...] = jnp.where(diagonal, 1.0, 0.0)
    sub = lax.broadcasted_iota(jnp.int32, (8, wide), 0)
    small = lax.broadcasted_iota(jnp.int32, (wide, wide), 0) == lax.broadcasted_iota(jnp.int32, (wide, wide), 1)
    tiles = wide // 8
    for block in range(order // wide):
        at = slice(block * wide, block * wide + wide)
        whole = s_ref[at, at]
        a = [whole[8 * t : 8 * t + 8, :] for t in range(tiles)]
        w = [jnp.where(small[8 * t : 8 * t + 8, :], 1.0, 0.0) for t in range(tiles)]
        for m in range(tiles):
            cols = {
                t: [jnp.broadcast_to(a[t][:, 8 * m + c : 8 * m + c + 1], (8, wide)) for c in range(8)]
                for t in range(m, tiles)
            }
            scale = jnp.zeros((8, wide), F32)
            for c in range(8):
                pivot = jnp.broadcast_to(cols[m][c][c : c + 1, :], (8, wide))
                root = lax.rsqrt(pivot)
                root = root * (1.5 - 0.5 * pivot * root * root)
                scale = jnp.where(sub == c, root, scale)
                less = root * root
                row_a = jnp.broadcast_to(a[m][c : c + 1, :], (8, wide))
                row_w = jnp.broadcast_to(w[m][c : c + 1, :], (8, wide))
                heads = [jnp.broadcast_to(cols[m][d][c : c + 1, :], (8, wide)) for d in range(c + 1, 8)]
                for t in range(m, tiles):
                    times = cols[t][c] * less
                    if t == m:
                        times = jnp.where(sub > c, times, 0.0)
                    a[t] = a[t] - times * row_a
                    w[t] = w[t] - times * row_w
                    for d in range(c + 1, 8):
                        cols[t][d] = cols[t][d] - times * heads[d - c - 1]
            w[m] = w[m] * scale
        low = jnp.concatenate(w, 0)
        row_inv = jnp.dot(low, inv_ref[at, :], precision=highest, preferred_element_type=F32)
        inv_ref[at, :] = row_inv
        if (block + 1) * wide < order:
            rest = slice((block + 1) * wide, order)
            row_s = jnp.dot(low, s_ref[at, rest], precision=highest, preferred_element_type=F32)
            s_ref[rest, rest] -= lax.dot_general(row_s, row_s, TN, precision=highest, preferred_element_type=F32)
            inv_ref[rest, :] -= lax.dot_general(row_s, row_inv, TN, precision=highest, preferred_element_type=F32)


def factor_call(ps):
    vmem = pl.BlockSpec(memory_space=pltpu.VMEM)
    return pl.pallas_call(
        factor_kernel,
        out_shape=jax.ShapeDtypeStruct(ps.shape, F32),
        in_specs=[vmem],
        out_specs=vmem,
        scratch_shapes=[pltpu.VMEM(ps.shape, F32)],
        compiler_params=pltpu.CompilerParams(vmem_limit_bytes=32 * 2**20),
        cost_estimate=pl.CostEstimate(flops=4 * 10**9, bytes_accessed=4 * 2**20, transcendentals=0),
        name="factor",
    )(ps)


def rows_kernel(
    pos_ref, at_ref, x_ref, y_ref, panel_ref, which_ref, place_ref, note_ref, cons_hbm, send_ref,
    a_ref, z_ref, e_ref, c_ref, zero_ref, one_ref, cons_ref, sem,
):
    step = pl.program_id(0)
    count = panel_ref.shape[0]
    parts = N // count
    tile = which_ref.shape[0]
    copy = pltpu.make_async_copy(cons_hbm, cons_ref, sem)

    @pl.when(step == 0)
    def _():
        copy.start()
        send_ref[...] = jnp.zeros_like(send_ref)
        send_ref[:, :128] = note_ref[...]

    @pl.when(step < parts)
    def _():
        form_blocks(step, count, pos_ref, at_ref, x_ref, y_ref, panel_ref, zero_ref, one_ref, a_ref, z_ref, e_ref, c_ref)

    @pl.when(step == parts)
    def _():
        copy.wait()

    @pl.when(step >= parts)
    def _():
        rows = pl.ds(pl.multiple_of((step - parts) * tile, 64), tile)
        cons = cons_ref[rows, :]
        out = jnp.where(which_ref[...] == 0, dot(cons, zero_ref[...], NT), dot(cons, one_ref[...], NT))
        hit = lax.broadcasted_iota(jnp.int32, (send_ref.shape[0], tile), 0) == place_ref[0]
        hit = jnp.where(hit, 1.0, 0.0).astype(BF16)
        high, rest = split(out)
        send_ref[...] += dot(hit, high) + dot(hit, rest)


def form_blocks(step, count, pos_ref, at_ref, x_ref, y_ref, panel_ref, zero_ref, one_ref, a_ref, z_ref, e_ref, c_ref):
    start = pl.multiple_of(step * count, count)

    def low(shape):
        return lax.broadcasted_iota(jnp.int32, shape, 1) < BS

    @pl.when(step == 0)
    def _():
        for s in range(2):
            rows = pl.ds(pl.multiple_of(at_ref[2 * s] * BS, BS), BS)
            first = low((BS, 128))
            for k in range(NB // 2):
                u = x_ref[rows, 128 * k : 128 * k + 128]
                v = y_ref[rows, 128 * k : 128 * k + 128]
                for p, both in (
                    (2 * k, jnp.where(first, u, pltpu.roll(v, BS, 1))),
                    (2 * k + 1, jnp.where(first, pltpu.roll(u, BS, 1), v)),
                ):
                    high, rest = split(both)
                    a_ref[p, s * BS : s * BS + BS, :] = high
                    a_ref[p, 128 + s * BS : 128 + s * BS + BS, :] = rest
        first = low((N, 128))
        for n, ref in enumerate((y_ref, x_ref)):
            halves = []
            for s in range(2):
                b = at_ref[2 * s + 1]
                tile = ref[:, pl.ds(pl.multiple_of(b // 2 * 128, 128), 128)]
                halves.append(jnp.where(b % 2 == s, tile, pltpu.roll(tile, BS, 1)))
            high, rest = split(jnp.where(first, halves[0], halves[1]))
            for q in range(NB):
                z_ref[q, :BS, 128 * n : 128 * n + 128] = high[q * BS : q * BS + BS]
                z_ref[q, BS:, 128 * n : 128 * n + 128] = rest[q * BS : q * BS + BS]

    first = low((8, 128))
    for k in range(BS // 2):
        pair = panel_ref[:, 128 * k : 128 * k + 128].astype(F32)
        for half in range(count // 8):
            u = pair[8 * half : 8 * half + 8]
            v = pltpu.roll(u, BS, 1)
            e_ref[pl.ds(512 * half + 2 * k, 8, stride=BS), :] = jnp.where(first, u, v)
            e_ref[pl.ds(512 * half + 2 * k + 1, 8, stride=BS), :] = jnp.where(first, v, u)

    keep = low((BS, 128))

    def group(g, carry):
        ones, twos, ps = [], [], []
        for n in range(16):
            j = g * 16 + n
            position = pos_ref[step * count + j]
            p = position // NB
            q = position % NB
            ps.append((p, q))
            ee = e_ref[slice(j * BS, j * BS + BS), :].astype(BF16)
            ones.append(dot(ee, z_ref[q]))
            twos.append(dot(jnp.concatenate([ee, ee], 0)[:, :BS], z_ref[p], TN))
        parts = []
        for one, two in zip(ones, twos):
            right = jnp.concatenate([one[:, :128], one[:, 128:], two[:, :128], two[:, 128:]], 0)
            parts.append(jnp.concatenate(split(right), 1))
        outs = []
        for (p, q), part in zip(ps, parts):
            outs.append(dot(jnp.concatenate([a_ref[p], a_ref[q]], 1), part))
        for n, out in enumerate(outs):
            here = out[:BS, :128] + (out[:BS, 128:] + out[128 : 128 + BS, :128])
            there = out[BS:128, :128] + (out[BS:128, 128:] + out[128 + BS :, :128])
            c_ref[slice((g * 16 + n) * BS, (g * 16 + n) * BS + BS), :] = jnp.where(keep, here, there)
        return carry

    def give(g):
        for k in range(BS // 2):
            firsts, seconds = [], []
            for half in range(16 // 8):
                u = c_ref[pl.ds(BS * 16 * g + 512 * half + 2 * k, 8, stride=BS), :]
                v = c_ref[pl.ds(BS * 16 * g + 512 * half + 2 * k + 1, 8, stride=BS), :]
                firsts.append(jnp.where(first, u, pltpu.roll(v, BS, 1)))
                seconds.append(jnp.where(first, pltpu.roll(u, BS, 1), v))
            rows = pl.ds(start + g * 16, 16)
            zero_ref[rows, 128 * k : 128 * k + 128] = jnp.concatenate(firsts, 0).astype(BF16)
            one_ref[rows, 128 * k : 128 * k + 128] = jnp.concatenate(seconds, 0).astype(BF16)

    group(0, 0)
    give(0)
    group(1, 0)
    give(1)


def rows_call(panel_pos, at, x_mat, y_inv, panel_blocks, which, place, note, cons):
    count = 32
    columns, flat = panel_blocks.shape
    slots = cons.shape[0]
    parts = columns // count
    tiles = place.shape[0]
    tile = slots // tiles
    smem = pl.BlockSpec(memory_space=pltpu.SMEM)
    vmem = pl.BlockSpec(memory_space=pltpu.VMEM)
    return pl.pallas_call(
        rows_kernel,
        grid=(parts + tiles,),
        out_shape=jax.ShapeDtypeStruct((note.shape[0], columns), F32),
        in_specs=[
            smem,
            smem,
            vmem,
            vmem,
            pl.BlockSpec((count, flat), lambda i: (jnp.minimum(i, parts - 1), 0)),
            pl.BlockSpec((tile, 1), lambda i: (jnp.maximum(i - parts, 0), 0)),
            pl.BlockSpec((1, 1, tile), lambda i: (jnp.maximum(i - parts, 0), 0, 0)),
            vmem,
            pl.BlockSpec(memory_space=pl.ANY),
        ],
        out_specs=vmem,
        scratch_shapes=[
            pltpu.VMEM((NB, 256, 128), BF16),
            pltpu.VMEM((NB, 128, 256), BF16),
            pltpu.VMEM((count * BS, 128), F32),
            pltpu.VMEM((count * BS, 128), F32),
            pltpu.VMEM((columns, flat), BF16),
            pltpu.VMEM((columns, flat), BF16),
            pltpu.VMEM((slots, flat), BF16),
            pltpu.SemaphoreType.DMA,
        ],
        compiler_params=pltpu.CompilerParams(vmem_limit_bytes=56 * 2**20),
        cost_estimate=pl.CostEstimate(flops=36 * 10**9, bytes_accessed=14 * 2**20, transcendentals=0),
        name="rows",
    )(panel_pos, at, x_mat, y_inv, panel_blocks, which, place, note, cons)


def finish_kernel(local_ref, recv_ref, inverse_ref, slab_ref, high_ref):
    hit = lax.broadcasted_iota(jnp.int32, (slab_ref.shape[0], recv_ref.shape[0]), 0) == local_ref[...]
    hit = jnp.where(hit, 1.0, 0.0).astype(BF16)
    high, rest = split(recv_ref[...])
    raw_high, raw_rest = split(dot(hit, high) + dot(hit, rest))
    inv_high, inv_rest = split(inverse_ref[...])
    slab = dot(raw_high, inv_high, NT) + (dot(raw_high, inv_rest, NT) + dot(raw_rest, inv_high, NT))
    slab_ref[...] = slab
    high_ref[...] = slab.astype(BF16)


def finish_call(local, recv, inverse, rows):
    vmem = pl.BlockSpec(memory_space=pltpu.VMEM)
    shape = (rows, recv.shape[1])
    return pl.pallas_call(
        finish_kernel,
        out_shape=(jax.ShapeDtypeStruct(shape, F32), jax.ShapeDtypeStruct(shape, BF16)),
        in_specs=[vmem] * 3,
        out_specs=(vmem, vmem),
        compiler_params=pltpu.CompilerParams(vmem_limit_bytes=32 * 2**20),
        name="finish",
    )(local, recv, inverse)


def gather_slabs(slab, me, cols):
    def send(value, to):
        return lax.ppermute(value, "col", [(c, to(c)) for c in range(cols)])

    def up(c):
        return (c + 2) % cols

    def down(c):
        return (c - 2) % cols

    def mate(c):
        return c ^ 1

    half = slab.shape[0] // 2
    before, after = send(slab, up), send(slab, down)
    across = (send(before[:half], up), send(after[half:], down))
    mine = [(slab,), (before,), (after,), across]
    theirs = [tuple(send(piece, mate) for piece in pieces) for pieces in mine]
    owners = [me, (me - 2) % cols, (me + 2) % cols, (me + 4) % cols]
    owners += [me ^ 1, ((me ^ 1) - 2) % cols, ((me ^ 1) + 2) % cols, ((me ^ 1) + 4) % cols]
    return mine + theirs, jnp.stack(owners)


def update_call(owners, picked, slabs, trailing):
    cut = [len(pieces) for pieces in slabs]
    flat = [piece for pieces in slabs for piece in pieces]
    rows = trailing.shape[0] // len(slabs)

    def kernel(owners_ref, picked_ref, *refs):
        trailing_ref, out_ref = refs[-2:]
        at = 0
        for n, many in enumerate(cut):
            pieces = refs[at : at + many]
            at += many

            @pl.when(pl.program_id(0) == n)
            def _(pieces=pieces):
                for k, piece in enumerate(pieces):
                    part = slice(k * piece.shape[0], (k + 1) * piece.shape[0])
                    out_ref[part, :] = trailing_ref[part, :] - dot(piece[...], picked_ref[...], NT)

    vmem = pl.BlockSpec(memory_space=pltpu.VMEM)
    block = pl.BlockSpec((rows, trailing.shape[1]), lambda i, owners_ref: (owners_ref[i], 0))
    return pl.pallas_call(
        kernel,
        grid_spec=pltpu.PrefetchScalarGridSpec(
            num_scalar_prefetch=1,
            grid=(len(slabs),),
            in_specs=[vmem] * (1 + len(flat)) + [block],
            out_specs=block,
        ),
        out_shape=jax.ShapeDtypeStruct(trailing.shape, F32),
        compiler_params=pltpu.CompilerParams(vmem_limit_bytes=32 * 2**20),
        name="update",
    )(owners, picked, *flat, trailing)


def row_id(position):
    return position % NB * NB + position // NB


def body(
    x_mat,
    y_inv,
    panel_blocks,
    panel_pos,
    group_blocks,
    cons_blocks,
    slot_block,
    slot_row,
    group_size,
    trailing,
):
    rows_size = lax.axis_size("row")
    cols_size = lax.axis_size("col")
    devices = rows_size * cols_size
    col_index = lax.axis_index("col")
    device_id = lax.axis_index("row") * cols_size + col_index
    panel_cols = panel_blocks.shape[0]
    own = panel_cols // devices
    slots = cons_blocks.shape[0]
    sub_rows = trailing.shape[0] // cols_size
    places = 8

    live = jnp.arange(slots, dtype=jnp.int32) < group_size[0]
    target = slot_row // sub_rows
    hits = ((target[:, None] == jnp.arange(devices, dtype=jnp.int32)[None, :]) & live[:, None]).astype(BF16)
    earlier = (
        lax.broadcasted_iota(jnp.int32, (slots, slots), 0) > lax.broadcasted_iota(jnp.int32, (slots, slots), 1)
    ).astype(BF16)
    rank = jnp.sum(dot(earlier, hits) * hits.astype(F32), axis=1).astype(jnp.int32)
    place = jnp.where(live, target * places + rank, -1)
    sends = lax.broadcasted_iota(jnp.int32, (devices * places, slots), 0) == place[None, :]
    local = jnp.sum(jnp.where(sends, (slot_row % sub_rows + 1)[None, :], 0), axis=1)
    note = jnp.pad(local.reshape(devices, places).astype(F32), ((0, 0), (0, 128 - places)))[:, None, :]
    note = jnp.where(jnp.arange(places)[None, :, None] == places - 1, note, 0.0).reshape(devices * places, 128)

    own_values = lax.dynamic_slice_in_dim(panel_blocks, device_id * own, own, 0).reshape(own, BS, BS)
    own_pos = lax.dynamic_slice_in_dim(panel_pos, device_id * own, own, 0)
    ps_rows = panel_call(own_pos, x_mat, y_inv, own_values, panel_blocks, row_id(panel_pos)[None, :])
    ps = lax.all_gather(ps_rows, AXES, axis=0, tiled=True)

    at = group_blocks[device_id]
    at = jnp.stack([at // NB, at % NB], 1).reshape(-1)
    send = rows_call(
        panel_pos, at, x_mat, y_inv, panel_blocks, slot_block[:, None], place.reshape(2, 1, -1), note, cons_blocks
    )
    recv = lax.all_to_all(send.reshape(devices, places, panel_cols), AXES, 0, 0, tiled=True)
    inverse = factor_call(ps)
    local = recv[:, places - 1, :places].astype(jnp.int32).reshape(1, -1) - 1
    slab, slab_high = finish_call(local, recv.reshape(devices * places, panel_cols), inverse, sub_rows)

    block_rows = trailing.shape[1] // rows_size
    lead = lax.all_to_all(slab_high[: block_rows * cols_size].reshape(cols_size, block_rows, panel_cols), "col", 0, 0, tiled=True)[0]
    picked = lax.all_to_all(jnp.broadcast_to(lead[None], (rows_size, block_rows, panel_cols)), "row", 0, 0, tiled=True)
    picked = picked.reshape(trailing.shape[1], panel_cols)
    slabs, owners = gather_slabs(slab_high, col_index, cols_size)
    updated = update_call(owners, picked, slabs, trailing)
    return (slab, updated)


def solution(mesh):
    return jax.shard_map(
        body,
        mesh=mesh,
        in_specs=(
            P(),
            P(),
            P(),
            P(),
            P(),
            P(("row", "col"), None),
            P(("row", "col")),
            P(("row", "col")),
            P(("row", "col")),
            P("row", "col"),
        ),
        out_specs=(P(("row", "col"), None), P("row", "col")),
        check_vma=False,
    )
```

```python
import math

import jax
import jax.numpy as jnp
from jax import lax
from jax.experimental import pallas as pl
from jax.experimental.pallas import tpu as pltpu
from jax.sharding import PartitionSpec as P

F32 = jnp.float32
BF16 = jnp.bfloat16
BS = 64
PITCH = 72
NB = 8
N = 512
AXES = ("row", "col")
NT = (((1,), (1,)), ((), ()))
TN = (((0,), (0,)), ((), ()))


def split(a):
    high = a.astype(BF16)
    return high, (a - high.astype(F32)).astype(BF16)


def dot(a, b, dims=(((1,), (0,)), ((), ()))):
    return lax.dot_general(a, b, dims, preferred_element_type=F32)


def panel_kernel(first_ref, pos_ref, x_ref, y_ref, e_ref, panel_hbm, rowid_ref, ps_ref, h_ref, t_ref, panel_ref, sem):
    copy = pltpu.make_async_copy(panel_hbm, panel_ref, sem)
    copy.start()
    count = e_ref.shape[0]
    lane = lax.broadcasted_iota(jnp.int32, (8, 128), 1)
    heads = []
    for j in range(count):
        position = pos_ref[first_ref[0] + j]
        p = pl.multiple_of(position // NB * BS, BS)
        q = pl.multiple_of(position % NB * BS, BS)
        e = e_ref[j]
        yh, yl = split(jnp.concatenate([y_ref[pl.ds(q, BS), :], y_ref[pl.ds(p, BS), :]], 0))
        ey = dot(e, yh[:BS]) + dot(e, yl[:BS])
        ety = dot(e, yh[BS:], TN) + dot(e, yl[BS:], TN)
        xh, xl = split(jnp.concatenate([x_ref[pl.ds(p, BS), :], x_ref[pl.ds(q, BS), :]], 0))
        vh, vl = split(jnp.concatenate([ey, ety], 0))
        heads.append((xh, xl, vh, vl))
    for j, (xh, xl, vh, vl) in enumerate(heads):
        ah = jnp.concatenate([xh, vh], 0)
        al = jnp.concatenate([xl, vl], 0)
        bh = jnp.concatenate([vh, xh], 0)
        bl = jnp.concatenate([vl, xl], 0)
        h = dot(ah, bh, TN) + (dot(ah, bl, TN) + dot(al, bh, TN))
        for b in range(NB // 2):
            for a in range(NB):
                h_ref[j, b, a * PITCH : a * PITCH + BS] = h[a * BS : a * BS + BS, b * 128 : b * 128 + 128]
    for j in range(count):
        for pair in range(BS // 2):
            r = pair * 2
            out = slice(pair * 128, pair * 128 + 128)
            for b in range(NB // 2):
                u = h_ref[j, b, pl.ds(r, NB, stride=PITCH), :]
                v = h_ref[j, b, pl.ds(r + 1, NB, stride=PITCH), :]
                even = jnp.where(lane < BS, u, pltpu.roll(v, BS, 1))
                odd = jnp.where(lane < BS, pltpu.roll(u, BS, 1), v)
                t_ref[j * 64 + 16 * b : j * 64 + 16 * b + 16, out] = jnp.concatenate([even, odd], 0).astype(BF16)
    copy.wait()
    hit = lax.broadcasted_iota(jnp.int32, (NB * NB, N), 0) == row_id(rowid_ref[...])
    all_blocks = dot(t_ref[...], panel_ref[...], NT)
    for j in range(count):
        part = all_blocks[j * 64 : j * 64 + 64, :]
        row = jnp.sum(jnp.where(hit, part, 0.0), axis=0, keepdims=True)
        for k in range(N // 128):
            ps_ref[j * (N // 128) + k : j * (N // 128) + k + 1, :] = row[:, k * 128 : k * 128 + 128]


def panel_call(first, panel_pos, x_mat, y_inv, own_e, panel_blocks):
    count = own_e.shape[0]
    vmem = pl.BlockSpec(memory_space=pltpu.VMEM)
    return pl.pallas_call(
        panel_kernel,
        out_shape=jax.ShapeDtypeStruct((count * N // 128, 128), F32),
        in_specs=[
            pl.BlockSpec(memory_space=pltpu.SMEM),
            pl.BlockSpec(memory_space=pltpu.SMEM),
            vmem,
            vmem,
            vmem,
            pl.BlockSpec(memory_space=pl.ANY),
            vmem,
        ],
        out_specs=vmem,
        scratch_shapes=[
            pltpu.VMEM((count, NB // 2, NB * PITCH, 2 * BS), F32),
            pltpu.VMEM((count * NB * NB, BS * BS), BF16),
            pltpu.VMEM(panel_blocks.shape, BF16),
            pltpu.SemaphoreType.DMA,
        ],
        compiler_params=pltpu.CompilerParams(vmem_limit_bytes=56 * 2**20),
        name="panel",
    )(first, panel_pos, x_mat, y_inv, own_e, panel_blocks, panel_pos[None, :])


def factor_kernel(ps_ref, inv_ref, s_ref):
    order = inv_ref.shape[0]
    wide = 128
    highest = lax.Precision.HIGHEST
    ps = jnp.concatenate([ps_ref[pl.ds(k, order, stride=order // 128), :] for k in range(order // 128)], 1)
    diagonal = lax.broadcasted_iota(jnp.int32, (order, order), 0) == lax.broadcasted_iota(jnp.int32, (order, order), 1)
    symmetric = 0.5 * (ps + ps.T)
    trace = jnp.sum(jnp.sum(jnp.where(diagonal, symmetric, 0.0), axis=1, keepdims=True), axis=0, keepdims=True)
    s_ref[...] = symmetric + jnp.where(diagonal, 0.01 / order * trace, 0.0)
    inv_ref[...] = jnp.where(diagonal, 1.0, 0.0)
    sub = lax.broadcasted_iota(jnp.int32, (8, wide), 0)
    small = lax.broadcasted_iota(jnp.int32, (wide, wide), 0) == lax.broadcasted_iota(jnp.int32, (wide, wide), 1)
    tiles = wide // 8
    for block in range(order // wide):
        at = slice(block * wide, block * wide + wide)
        whole = s_ref[at, at]
        a = [whole[8 * t : 8 * t + 8, :] for t in range(tiles)]
        w = [jnp.where(small[8 * t : 8 * t + 8, :], 1.0, 0.0) for t in range(tiles)]
        for m in range(tiles):
            cols = {
                t: [jnp.broadcast_to(a[t][:, 8 * m + c : 8 * m + c + 1], (8, wide)) for c in range(8)]
                for t in range(m, tiles)
            }
            scale = jnp.zeros((8, wide), F32)
            for c in range(8):
                pivot = jnp.broadcast_to(cols[m][c][c : c + 1, :], (8, wide))
                root = lax.rsqrt(pivot)
                root = root * (1.5 - 0.5 * pivot * root * root)
                scale = jnp.where(sub == c, root, scale)
                less = root * root
                row_a = jnp.broadcast_to(a[m][c : c + 1, :], (8, wide))
                row_w = jnp.broadcast_to(w[m][c : c + 1, :], (8, wide))
                heads = [jnp.broadcast_to(cols[m][d][c : c + 1, :], (8, wide)) for d in range(c + 1, 8)]
                for t in range(m, tiles):
                    times = cols[t][c] * less
                    if t == m:
                        times = jnp.where(sub > c, times, 0.0)
                    a[t] = a[t] - times * row_a
                    w[t] = w[t] - times * row_w
                    for d in range(c + 1, 8):
                        cols[t][d] = cols[t][d] - times * heads[d - c - 1]
            w[m] = w[m] * scale
        low = jnp.concatenate(w, 0)
        row_inv = jnp.dot(low, inv_ref[at, :], precision=highest, preferred_element_type=F32)
        inv_ref[at, :] = row_inv
        if (block + 1) * wide < order:
            rest = slice((block + 1) * wide, order)
            row_s = jnp.dot(low, s_ref[at, rest], precision=highest, preferred_element_type=F32)
            s_ref[rest, rest] -= lax.dot_general(row_s, row_s, TN, precision=highest, preferred_element_type=F32)
            inv_ref[rest, :] -= lax.dot_general(row_s, row_inv, TN, precision=highest, preferred_element_type=F32)


def factor_call(ps):
    order = math.isqrt(ps.size)
    vmem = pl.BlockSpec(memory_space=pltpu.VMEM)
    return pl.pallas_call(
        factor_kernel,
        out_shape=jax.ShapeDtypeStruct((order, order), F32),
        in_specs=[vmem],
        out_specs=vmem,
        scratch_shapes=[pltpu.VMEM((order, order), F32)],
        compiler_params=pltpu.CompilerParams(vmem_limit_bytes=32 * 2**20),
        cost_estimate=pl.CostEstimate(flops=4 * 10**9, bytes_accessed=4 * 2**20, transcendentals=0),
        name="factor",
    )(ps)


def rows_kernel(
    pos_ref, at_ref, x_ref, y_ref, panel_ref, which_ref, place_ref, note_ref, cons_hbm, send_ref,
    a_ref, z_ref, e_ref, c_ref, zero_ref, one_ref, cons_ref, sem,
):
    step = pl.program_id(0)
    count = panel_ref.shape[0]
    parts = N // count
    tile = which_ref.shape[0]
    copy = pltpu.make_async_copy(cons_hbm, cons_ref, sem)

    @pl.when(step == 0)
    def _():
        copy.start()
        send_ref[...] = jnp.zeros_like(send_ref)
        send_ref[:, :128] = note_ref[...]

    @pl.when(step < parts)
    def _():
        form_blocks(step, count, pos_ref, at_ref, x_ref, y_ref, panel_ref, zero_ref, one_ref, a_ref, z_ref, e_ref, c_ref)

    @pl.when(step == parts)
    def _():
        copy.wait()

    @pl.when(step >= parts)
    def _():
        rows = pl.ds(pl.multiple_of((step - parts) * tile, 64), tile)
        cons = cons_ref[rows, :]
        out = jnp.where(which_ref[...] == 0, dot(cons, zero_ref[...], NT), dot(cons, one_ref[...], NT))
        hit = lax.broadcasted_iota(jnp.int32, (send_ref.shape[0], tile), 0) == place_ref[0]
        hit = jnp.where(hit, 1.0, 0.0).astype(BF16)
        high, rest = split(out)
        send_ref[...] += dot(hit, high) + dot(hit, rest)


def form_blocks(step, count, pos_ref, at_ref, x_ref, y_ref, panel_ref, zero_ref, one_ref, a_ref, z_ref, e_ref, c_ref):
    start = pl.multiple_of(step * count, count)

    def low(shape):
        return lax.broadcasted_iota(jnp.int32, shape, 1) < BS

    @pl.when(step == 0)
    def _():
        for s in range(2):
            rows = pl.ds(pl.multiple_of(at_ref[2 * s] * BS, BS), BS)
            first = low((BS, 128))
            for k in range(NB // 2):
                u = x_ref[rows, 128 * k : 128 * k + 128]
                v = y_ref[rows, 128 * k : 128 * k + 128]
                for p, both in (
                    (2 * k, jnp.where(first, u, pltpu.roll(v, BS, 1))),
                    (2 * k + 1, jnp.where(first, pltpu.roll(u, BS, 1), v)),
                ):
                    high, rest = split(both)
                    a_ref[p, s * BS : s * BS + BS, :] = high
                    a_ref[p, 128 + s * BS : 128 + s * BS + BS, :] = rest
        first = low((N, 128))
        for n, ref in enumerate((y_ref, x_ref)):
            halves = []
            for s in range(2):
                b = at_ref[2 * s + 1]
                tile = ref[:, pl.ds(pl.multiple_of(b // 2 * 128, 128), 128)]
                halves.append(jnp.where(b % 2 == s, tile, pltpu.roll(tile, BS, 1)))
            high, rest = split(jnp.where(first, halves[0], halves[1]))
            for q in range(NB):
                z_ref[q, :BS, 128 * n : 128 * n + 128] = high[q * BS : q * BS + BS]
                z_ref[q, BS:, 128 * n : 128 * n + 128] = rest[q * BS : q * BS + BS]

    first = low((8, 128))
    for k in range(BS // 2):
        pair = panel_ref[:, 128 * k : 128 * k + 128].astype(F32)
        for half in range(count // 8):
            u = pair[8 * half : 8 * half + 8]
            v = pltpu.roll(u, BS, 1)
            e_ref[pl.ds(8 * PITCH * half + 2 * k, 8, stride=PITCH), :] = jnp.where(first, u, v)
            e_ref[pl.ds(8 * PITCH * half + 2 * k + 1, 8, stride=PITCH), :] = jnp.where(first, v, u)

    keep = low((BS, 128))

    def group(g, carry):
        ones, twos, ps = [], [], []
        for n in range(16):
            j = g * 16 + n
            position = pos_ref[step * count + j]
            p = position // NB
            q = position % NB
            ps.append((p, q))
            ee = e_ref[slice(j * PITCH, j * PITCH + BS), :].astype(BF16)
            ones.append(dot(ee, z_ref[q]))
            twos.append(dot(jnp.concatenate([ee, ee], 0)[:, :BS], z_ref[p], TN))
        parts = []
        for one, two in zip(ones, twos):
            right = jnp.concatenate([one[:, :128], one[:, 128:], two[:, :128], two[:, 128:]], 0)
            parts.append(jnp.concatenate(split(right), 1))
        outs = []
        for (p, q), part in zip(ps, parts):
            outs.append(dot(jnp.concatenate([a_ref[p], a_ref[q]], 1), part))
        for n, out in enumerate(outs):
            here = out[:BS, :128] + (out[:BS, 128:] + out[128 : 128 + BS, :128])
            there = out[BS:128, :128] + (out[BS:128, 128:] + out[128 + BS :, :128])
            c_ref[slice((g * 16 + n) * PITCH, (g * 16 + n) * PITCH + BS), :] = jnp.where(keep, here, there)
        return carry

    def give(g):
        for k in range(BS // 2):
            firsts, seconds = [], []
            for half in range(16 // 8):
                u = c_ref[pl.ds(PITCH * (16 * g + 8 * half) + 2 * k, 8, stride=PITCH), :]
                v = c_ref[pl.ds(PITCH * (16 * g + 8 * half) + 2 * k + 1, 8, stride=PITCH), :]
                firsts.append(jnp.where(first, u, pltpu.roll(v, BS, 1)))
                seconds.append(jnp.where(first, pltpu.roll(u, BS, 1), v))
            rows = pl.ds(start + g * 16, 16)
            zero_ref[rows, 128 * k : 128 * k + 128] = jnp.concatenate(firsts, 0).astype(BF16)
            one_ref[rows, 128 * k : 128 * k + 128] = jnp.concatenate(seconds, 0).astype(BF16)

    group(0, 0)
    give(0)
    group(1, 0)
    give(1)


def rows_call(panel_pos, at, x_mat, y_inv, panel_blocks, which, place, note, cons):
    count = 32
    columns, flat = panel_blocks.shape
    slots = cons.shape[0]
    parts = columns // count
    tiles = place.shape[0]
    tile = slots // tiles
    smem = pl.BlockSpec(memory_space=pltpu.SMEM)
    vmem = pl.BlockSpec(memory_space=pltpu.VMEM)
    return pl.pallas_call(
        rows_kernel,
        grid=(parts + tiles,),
        out_shape=jax.ShapeDtypeStruct((note.shape[0], columns), F32),
        in_specs=[
            smem,
            smem,
            vmem,
            vmem,
            pl.BlockSpec((count, flat), lambda i: (jnp.minimum(i, parts - 1), 0)),
            pl.BlockSpec((tile, 1), lambda i: (jnp.maximum(i - parts, 0), 0)),
            pl.BlockSpec((1, 1, tile), lambda i: (jnp.maximum(i - parts, 0), 0, 0)),
            vmem,
            pl.BlockSpec(memory_space=pl.ANY),
        ],
        out_specs=vmem,
        scratch_shapes=[
            pltpu.VMEM((NB, 256, 128), BF16),
            pltpu.VMEM((NB, 128, 256), BF16),
            pltpu.VMEM((count * PITCH, 128), F32),
            pltpu.VMEM((count * PITCH, 128), F32),
            pltpu.VMEM((columns, flat), BF16),
            pltpu.VMEM((columns, flat), BF16),
            pltpu.VMEM((slots, flat), BF16),
            pltpu.SemaphoreType.DMA,
        ],
        compiler_params=pltpu.CompilerParams(vmem_limit_bytes=56 * 2**20),
        cost_estimate=pl.CostEstimate(flops=36 * 10**9, bytes_accessed=14 * 2**20, transcendentals=0),
        name="rows",
    )(panel_pos, at, x_mat, y_inv, panel_blocks, which, place, note, cons)


def finish_kernel(local_ref, recv_ref, inverse_ref, slab_ref, high_ref):
    hit = lax.broadcasted_iota(jnp.int32, (slab_ref.shape[0], recv_ref.shape[0]), 0) == local_ref[...]
    hit = jnp.where(hit, 1.0, 0.0).astype(BF16)
    high, rest = split(recv_ref[...])
    raw_high, raw_rest = split(dot(hit, high) + dot(hit, rest))
    inv_high, inv_rest = split(inverse_ref[...])
    slab = dot(raw_high, inv_high, NT) + (dot(raw_high, inv_rest, NT) + dot(raw_rest, inv_high, NT))
    slab_ref[...] = slab
    high_ref[...] = slab.astype(BF16)


def finish_call(local, recv, inverse, rows):
    vmem = pl.BlockSpec(memory_space=pltpu.VMEM)
    shape = (rows, recv.shape[1])
    return pl.pallas_call(
        finish_kernel,
        out_shape=(jax.ShapeDtypeStruct(shape, F32), jax.ShapeDtypeStruct(shape, BF16)),
        in_specs=[vmem] * 3,
        out_specs=(vmem, vmem),
        compiler_params=pltpu.CompilerParams(vmem_limit_bytes=32 * 2**20),
        name="finish",
    )(local, recv, inverse)


def row_id(position):
    return position % NB * NB + position // NB


def body(
    x_mat,
    y_inv,
    panel_blocks,
    panel_pos,
    group_blocks,
    cons_blocks,
    slot_block,
    slot_row,
    group_size,
    trailing,
):
    rows_size = lax.axis_size("row")
    cols_size = lax.axis_size("col")
    devices = rows_size * cols_size
    col_index = lax.axis_index("col")
    device_id = lax.axis_index("row") * cols_size + col_index
    panel_cols = panel_blocks.shape[0]
    own = panel_cols // devices
    slots = cons_blocks.shape[0]
    sub_rows = trailing.shape[0] // cols_size
    places = 8

    live = jnp.arange(slots, dtype=jnp.int32) < group_size[0]
    target = slot_row // sub_rows
    hits = ((target[:, None] == jnp.arange(devices, dtype=jnp.int32)[None, :]) & live[:, None]).astype(BF16)
    earlier = (
        lax.broadcasted_iota(jnp.int32, (slots, slots), 0) > lax.broadcasted_iota(jnp.int32, (slots, slots), 1)
    ).astype(BF16)
    rank = jnp.sum(dot(earlier, hits) * hits.astype(F32), axis=1).astype(jnp.int32)
    place = jnp.where(live, target * places + rank, -1)
    sends = lax.broadcasted_iota(jnp.int32, (devices * places, slots), 0) == place[None, :]
    local = jnp.sum(jnp.where(sends, (slot_row % sub_rows + 1)[None, :], 0), axis=1)
    note = jnp.pad(local.reshape(devices, places).astype(F32), ((0, 0), (0, 128 - places)))[:, None, :]
    note = jnp.where(jnp.arange(places)[None, :, None] == places - 1, note, 0.0).reshape(devices * places, 128)

    own_values = lax.dynamic_slice_in_dim(panel_blocks, device_id * own, own, 0).reshape(own, BS, BS)
    first = jnp.full((1,), device_id * own, jnp.int32)
    ps_rows = panel_call(first, panel_pos, x_mat, y_inv, own_values, panel_blocks)
    ps = lax.all_gather(ps_rows, AXES, axis=0, tiled=True)

    at = group_blocks[device_id]
    at = jnp.stack([at // NB, at % NB], 1).reshape(-1)
    send = rows_call(
        panel_pos, at, x_mat, y_inv, panel_blocks, slot_block[:, None], place.reshape(2, 1, -1), note, cons_blocks
    )
    recv = lax.all_to_all(send.reshape(devices, places, panel_cols), AXES, 0, 0, tiled=True)
    inverse = factor_call(ps)
    local = recv[:, places - 1, :places].astype(jnp.int32).reshape(1, -1) - 1
    slab, slab_high = finish_call(local, recv.reshape(devices * places, panel_cols), inverse, sub_rows)

    block_rows = trailing.shape[1] // rows_size
    lead = slab_high[: block_rows * cols_size].reshape(cols_size, block_rows, panel_cols)
    lead = lax.all_to_all(lead, "col", 0, 0, tiled=True)[0]
    picked = lax.all_to_all(jnp.broadcast_to(lead[None], (rows_size, block_rows, panel_cols)), "row", 0, 0, tiled=True)
    picked = picked.reshape(trailing.shape[1], panel_cols)
    all_rows = lax.all_gather(slab_high, "col", axis=0, tiled=True)
    updated = trailing - dot(all_rows, picked, NT)
    return (slab, updated)


def solution(mesh):
    return jax.shard_map(
        body,
        mesh=mesh,
        in_specs=(
            P(),
            P(),
            P(),
            P(),
            P(),
            P(("row", "col"), None),
            P(("row", "col")),
            P(("row", "col")),
            P(("row", "col")),
            P("row", "col"),
        ),
        out_specs=(P(("row", "col"), None), P("row", "col")),
        check_vma=False,
    )
```

```python
import math

import jax
import jax.numpy as jnp
from jax import lax
from jax.experimental import pallas as pl
from jax.experimental.pallas import tpu as pltpu
from jax.sharding import PartitionSpec as P

F32 = jnp.float32
BF16 = jnp.bfloat16
BS = 64
PITCH = 72
NB = 8
N = 512
AXES = ("row", "col")
NT = (((1,), (1,)), ((), ()))
TN = (((0,), (0,)), ((), ()))


def split(a):
    high = a.astype(BF16)
    return high, (a - high.astype(F32)).astype(BF16)


def dot(a, b, dims=(((1,), (0,)), ((), ()))):
    return lax.dot_general(a, b, dims, preferred_element_type=F32)


def panel_kernel(first_ref, pos_ref, x_ref, y_ref, e_ref, panel_hbm, rowid_ref, ps_ref, h_ref, t_ref, panel_ref, sem):
    copy = pltpu.make_async_copy(panel_hbm, panel_ref, sem)
    copy.start()
    count = e_ref.shape[0]
    lane = lax.broadcasted_iota(jnp.int32, (8, 128), 1)
    heads = []
    for j in range(count):
        position = pos_ref[first_ref[0] + j]
        p = pl.multiple_of(position // NB * BS, BS)
        q = pl.multiple_of(position % NB * BS, BS)
        e = e_ref[j]
        yh, yl = split(jnp.concatenate([y_ref[pl.ds(q, BS), :], y_ref[pl.ds(p, BS), :]], 0))
        ey = dot(e, yh[:BS]) + dot(e, yl[:BS])
        ety = dot(e, yh[BS:], TN) + dot(e, yl[BS:], TN)
        xh, xl = split(jnp.concatenate([x_ref[pl.ds(p, BS), :], x_ref[pl.ds(q, BS), :]], 0))
        vh, vl = split(jnp.concatenate([ey, ety], 0))
        heads.append((xh, xl, vh, vl))
    for j, (xh, xl, vh, vl) in enumerate(heads):
        ah = jnp.concatenate([xh, vh], 0)
        al = jnp.concatenate([xl, vl], 0)
        bh = jnp.concatenate([vh, xh], 0)
        bl = jnp.concatenate([vl, xl], 0)
        h = dot(ah, bh, TN) + (dot(ah, bl, TN) + dot(al, bh, TN))
        for b in range(NB // 2):
            for a in range(NB):
                h_ref[j, b, a * PITCH : a * PITCH + BS] = h[a * BS : a * BS + BS, b * 128 : b * 128 + 128]
    for j in range(count):
        for pair in range(BS // 2):
            r = pair * 2
            out = slice(pair * 128, pair * 128 + 128)
            for b in range(NB // 2):
                u = h_ref[j, b, pl.ds(r, NB, stride=PITCH), :]
                v = h_ref[j, b, pl.ds(r + 1, NB, stride=PITCH), :]
                even = jnp.where(lane < BS, u, pltpu.roll(v, BS, 1))
                odd = jnp.where(lane < BS, pltpu.roll(u, BS, 1), v)
                t_ref[j * 64 + 16 * b : j * 64 + 16 * b + 16, out] = jnp.concatenate([even, odd], 0).astype(BF16)
    copy.wait()
    hit = lax.broadcasted_iota(jnp.int32, (NB * NB, N), 0) == row_id(rowid_ref[...])
    all_blocks = dot(t_ref[...], panel_ref[...], NT)
    for j in range(count):
        part = all_blocks[j * 64 : j * 64 + 64, :]
        row = jnp.sum(jnp.where(hit, part, 0.0), axis=0, keepdims=True)
        for k in range(N // 128):
            ps_ref[j * (N // 128) + k : j * (N // 128) + k + 1, :] = row[:, k * 128 : k * 128 + 128]


def panel_call(first, panel_pos, x_mat, y_inv, own_e, panel_blocks):
    count = own_e.shape[0]
    vmem = pl.BlockSpec(memory_space=pltpu.VMEM)
    return pl.pallas_call(
        panel_kernel,
        out_shape=jax.ShapeDtypeStruct((count * N // 128, 128), F32),
        in_specs=[
            pl.BlockSpec(memory_space=pltpu.SMEM),
            pl.BlockSpec(memory_space=pltpu.SMEM),
            vmem,
            vmem,
            vmem,
            pl.BlockSpec(memory_space=pl.ANY),
            vmem,
        ],
        out_specs=vmem,
        scratch_shapes=[
            pltpu.VMEM((count, NB // 2, NB * PITCH, 2 * BS), F32),
            pltpu.VMEM((count * NB * NB, BS * BS), BF16),
            pltpu.VMEM(panel_blocks.shape, BF16),
            pltpu.SemaphoreType.DMA,
        ],
        compiler_params=pltpu.CompilerParams(vmem_limit_bytes=56 * 2**20),
        name="panel",
    )(first, panel_pos, x_mat, y_inv, own_e, panel_blocks, panel_pos[None, :])


def factor_kernel(ps_ref, inv_ref, s_ref):
    order = inv_ref.shape[0]
    wide = 128
    highest = lax.Precision.HIGHEST
    ps = jnp.concatenate([ps_ref[pl.ds(k, order, stride=order // 128), :] for k in range(order // 128)], 1)
    diagonal = lax.broadcasted_iota(jnp.int32, (order, order), 0) == lax.broadcasted_iota(jnp.int32, (order, order), 1)
    symmetric = 0.5 * (ps + ps.T)
    trace = jnp.sum(jnp.sum(jnp.where(diagonal, symmetric, 0.0), axis=1, keepdims=True), axis=0, keepdims=True)
    s_ref[...] = symmetric + jnp.where(diagonal, 0.01 / order * trace, 0.0)
    inv_ref[...] = jnp.where(diagonal, 1.0, 0.0)
    sub = lax.broadcasted_iota(jnp.int32, (8, wide), 0)
    small = lax.broadcasted_iota(jnp.int32, (wide, wide), 0) == lax.broadcasted_iota(jnp.int32, (wide, wide), 1)
    tiles = wide // 8
    for block in range(order // wide):
        at = slice(block * wide, block * wide + wide)
        whole = s_ref[at, at]
        a = [whole[8 * t : 8 * t + 8, :] for t in range(tiles)]
        w = [jnp.where(small[8 * t : 8 * t + 8, :], 1.0, 0.0) for t in range(tiles)]
        for m in range(tiles):
            cols = {
                t: [jnp.broadcast_to(a[t][:, 8 * m + c : 8 * m + c + 1], (8, wide)) for c in range(8)]
                for t in range(m, tiles)
            }
            scale = jnp.zeros((8, wide), F32)
            for c in range(8):
                pivot = jnp.broadcast_to(cols[m][c][c : c + 1, :], (8, wide))
                root = lax.rsqrt(pivot)
                root = root * (1.5 - 0.5 * pivot * root * root)
                scale = jnp.where(sub == c, root, scale)
                less = root * root
                row_a = jnp.broadcast_to(a[m][c : c + 1, :], (8, wide))
                row_w = jnp.broadcast_to(w[m][c : c + 1, :], (8, wide))
                heads = [jnp.broadcast_to(cols[m][d][c : c + 1, :], (8, wide)) for d in range(c + 1, 8)]
                for t in range(m, tiles):
                    times = cols[t][c] * less
                    if t == m:
                        times = jnp.where(sub > c, times, 0.0)
                    a[t] = a[t] - times * row_a
                    w[t] = w[t] - times * row_w
                    for d in range(c + 1, 8):
                        cols[t][d] = cols[t][d] - times * heads[d - c - 1]
            w[m] = w[m] * scale
        low = jnp.concatenate(w, 0)
        row_inv = jnp.dot(low, inv_ref[at, :], precision=highest, preferred_element_type=F32)
        inv_ref[at, :] = row_inv
        if (block + 1) * wide < order:
            rest = slice((block + 1) * wide, order)
            row_s = jnp.dot(low, s_ref[at, rest], precision=highest, preferred_element_type=F32)
            s_ref[rest, rest] -= lax.dot_general(row_s, row_s, TN, precision=highest, preferred_element_type=F32)
            inv_ref[rest, :] -= lax.dot_general(row_s, row_inv, TN, precision=highest, preferred_element_type=F32)


def factor_call(ps):
    order = math.isqrt(ps.size)
    vmem = pl.BlockSpec(memory_space=pltpu.VMEM)
    return pl.pallas_call(
        factor_kernel,
        out_shape=jax.ShapeDtypeStruct((order, order), F32),
        in_specs=[vmem],
        out_specs=vmem,
        scratch_shapes=[pltpu.VMEM((order, order), F32)],
        compiler_params=pltpu.CompilerParams(vmem_limit_bytes=32 * 2**20),
        cost_estimate=pl.CostEstimate(flops=4 * 10**9, bytes_accessed=4 * 2**20, transcendentals=0),
        name="factor",
    )(ps)


def rows_kernel(
    pos_ref, at_ref, x_ref, y_ref, panel_ref, which_ref, place_ref, note_ref, cons_hbm, send_ref,
    a_ref, z_ref, e_ref, c_ref, zero_ref, one_ref, cons_ref, sem,
):
    step = pl.program_id(0)
    count = panel_ref.shape[0]
    parts = N // count
    copy = pltpu.make_async_copy(cons_hbm, cons_ref, sem)

    @pl.when(step == 0)
    def _():
        copy.start()

    @pl.when(step < parts)
    def _():
        form_blocks(step, count, pos_ref, at_ref, x_ref, y_ref, panel_ref, zero_ref, one_ref, a_ref, z_ref, e_ref, c_ref)

    @pl.when(step == parts)
    def _():
        copy.wait()
        cons = cons_ref[...]
        out = jnp.where(which_ref[...] == 0, dot(cons, zero_ref[...], NT), dot(cons, one_ref[...], NT))
        hit = lax.broadcasted_iota(jnp.int32, (send_ref.shape[0], cons.shape[0]), 0) == place_ref[...]
        hit = jnp.where(hit, 1.0, 0.0).astype(BF16)
        high, rest = split(out)
        send_ref[...] = dot(hit, high) + dot(hit, rest)
        send_ref[:, :128] += note_ref[...]


def form_blocks(step, count, pos_ref, at_ref, x_ref, y_ref, panel_ref, zero_ref, one_ref, a_ref, z_ref, e_ref, c_ref):
    start = pl.multiple_of(step * count, count)

    def low(shape):
        return lax.broadcasted_iota(jnp.int32, shape, 1) < BS

    @pl.when(step == 0)
    def _():
        for s in range(2):
            rows = pl.ds(pl.multiple_of(at_ref[s] // NB * BS, BS), BS)
            first = low((BS, 128))
            for k in range(NB // 2):
                u = x_ref[rows, 128 * k : 128 * k + 128]
                v = y_ref[rows, 128 * k : 128 * k + 128]
                for p, both in (
                    (2 * k, jnp.where(first, u, pltpu.roll(v, BS, 1))),
                    (2 * k + 1, jnp.where(first, pltpu.roll(u, BS, 1), v)),
                ):
                    high, rest = split(both)
                    a_ref[p, s * BS : s * BS + BS, :] = high
                    a_ref[p, 128 + s * BS : 128 + s * BS + BS, :] = rest
        first = low((N, 128))
        for n, ref in enumerate((y_ref, x_ref)):
            halves = []
            for s in range(2):
                b = at_ref[s] % NB
                tile = ref[:, pl.ds(pl.multiple_of(b // 2 * 128, 128), 128)]
                halves.append(jnp.where(b % 2 == s, tile, pltpu.roll(tile, BS, 1)))
            high, rest = split(jnp.where(first, halves[0], halves[1]))
            for q in range(NB):
                z_ref[q, :BS, 128 * n : 128 * n + 128] = high[q * BS : q * BS + BS]
                z_ref[q, BS:, 128 * n : 128 * n + 128] = rest[q * BS : q * BS + BS]

    first = low((8, 128))
    for k in range(BS // 2):
        pair = panel_ref[:, 128 * k : 128 * k + 128].astype(F32)
        for half in range(count // 8):
            u = pair[8 * half : 8 * half + 8]
            v = pltpu.roll(u, BS, 1)
            e_ref[pl.ds(8 * PITCH * half + 2 * k, 8, stride=PITCH), :] = jnp.where(first, u, v)
            e_ref[pl.ds(8 * PITCH * half + 2 * k + 1, 8, stride=PITCH), :] = jnp.where(first, v, u)

    keep = low((BS, 128))

    def group(g, carry):
        ones, twos, ps = [], [], []
        for n in range(16):
            j = g * 16 + n
            position = pos_ref[step * count + j]
            p = position // NB
            q = position % NB
            ps.append((p, q))
            ee = e_ref[slice(j * PITCH, j * PITCH + BS), :].astype(BF16)
            ones.append(dot(ee, z_ref[q]))
            twos.append(dot(jnp.concatenate([ee, ee], 0)[:, :BS], z_ref[p], TN))
        parts = []
        for one, two in zip(ones, twos):
            right = jnp.concatenate([one[:, :128], one[:, 128:], two[:, :128], two[:, 128:]], 0)
            parts.append(jnp.concatenate(split(right), 1))
        outs = []
        for (p, q), part in zip(ps, parts):
            outs.append(dot(jnp.concatenate([a_ref[p], a_ref[q]], 1), part))
        for n, out in enumerate(outs):
            here = out[:BS, :128] + (out[:BS, 128:] + out[128 : 128 + BS, :128])
            there = out[BS:128, :128] + (out[BS:128, 128:] + out[128 + BS :, :128])
            c_ref[slice((g * 16 + n) * PITCH, (g * 16 + n) * PITCH + BS), :] = jnp.where(keep, here, there)
        return carry

    def give(g):
        for k in range(BS // 2):
            firsts, seconds = [], []
            for half in range(16 // 8):
                u = c_ref[pl.ds(PITCH * (16 * g + 8 * half) + 2 * k, 8, stride=PITCH), :]
                v = c_ref[pl.ds(PITCH * (16 * g + 8 * half) + 2 * k + 1, 8, stride=PITCH), :]
                firsts.append(jnp.where(first, u, pltpu.roll(v, BS, 1)))
                seconds.append(jnp.where(first, pltpu.roll(u, BS, 1), v))
            rows = pl.ds(start + g * 16, 16)
            zero_ref[rows, 128 * k : 128 * k + 128] = jnp.concatenate(firsts, 0).astype(BF16)
            one_ref[rows, 128 * k : 128 * k + 128] = jnp.concatenate(seconds, 0).astype(BF16)

    group(0, 0)
    give(0)
    group(1, 0)
    give(1)
    group(2, 0)
    give(2)
    group(3, 0)
    give(3)


def rows_call(panel_pos, at, x_mat, y_inv, panel_blocks, which, place, note, cons):
    count = 64
    columns, flat = panel_blocks.shape
    slots = cons.shape[0]
    parts = columns // count
    smem = pl.BlockSpec(memory_space=pltpu.SMEM)
    vmem = pl.BlockSpec(memory_space=pltpu.VMEM)
    return pl.pallas_call(
        rows_kernel,
        grid=(parts + 1,),
        out_shape=jax.ShapeDtypeStruct((note.shape[0], columns), F32),
        in_specs=[
            smem,
            smem,
            vmem,
            vmem,
            pl.BlockSpec((count, flat), lambda i: (jnp.minimum(i, parts - 1), 0)),
            vmem,
            vmem,
            vmem,
            pl.BlockSpec(memory_space=pl.ANY),
        ],
        out_specs=vmem,
        scratch_shapes=[
            pltpu.VMEM((NB, 256, 128), BF16),
            pltpu.VMEM((NB, 128, 256), BF16),
            pltpu.VMEM((count * PITCH, 128), F32),
            pltpu.VMEM((count * PITCH, 128), F32),
            pltpu.VMEM((columns, flat), BF16),
            pltpu.VMEM((columns, flat), BF16),
            pltpu.VMEM((slots, flat), BF16),
            pltpu.SemaphoreType.DMA,
        ],
        compiler_params=pltpu.CompilerParams(vmem_limit_bytes=56 * 2**20),
        cost_estimate=pl.CostEstimate(flops=36 * 10**9, bytes_accessed=14 * 2**20, transcendentals=0),
        name="rows",
    )(panel_pos, at, x_mat, y_inv, panel_blocks, which, place, note, cons)


def finish_kernel(local_ref, recv_ref, inverse_ref, slab_ref, high_ref):
    hit = lax.broadcasted_iota(jnp.int32, (slab_ref.shape[0], recv_ref.shape[0]), 0) == local_ref[...]
    hit = jnp.where(hit, 1.0, 0.0).astype(BF16)
    high, rest = split(recv_ref[...])
    raw_high, raw_rest = split(dot(hit, high) + dot(hit, rest))
    inv_high, inv_rest = split(inverse_ref[...])
    slab = dot(raw_high, inv_high, NT) + (dot(raw_high, inv_rest, NT) + dot(raw_rest, inv_high, NT))
    slab_ref[...] = slab
    high_ref[...] = slab.astype(BF16)


def finish_call(local, recv, inverse, rows):
    vmem = pl.BlockSpec(memory_space=pltpu.VMEM)
    shape = (rows, recv.shape[1])
    return pl.pallas_call(
        finish_kernel,
        out_shape=(jax.ShapeDtypeStruct(shape, F32), jax.ShapeDtypeStruct(shape, BF16)),
        in_specs=[vmem] * 3,
        out_specs=(vmem, vmem),
        compiler_params=pltpu.CompilerParams(vmem_limit_bytes=32 * 2**20),
        name="finish",
    )(local, recv, inverse)


def row_id(position):
    return position % NB * NB + position // NB


def body(
    x_mat,
    y_inv,
    panel_blocks,
    panel_pos,
    group_blocks,
    cons_blocks,
    slot_block,
    slot_row,
    group_size,
    trailing,
):
    rows_size = lax.axis_size("row")
    cols_size = lax.axis_size("col")
    devices = rows_size * cols_size
    col_index = lax.axis_index("col")
    device_id = lax.axis_index("row") * cols_size + col_index
    panel_cols = panel_blocks.shape[0]
    own = panel_cols // devices
    slots = cons_blocks.shape[0]
    sub_rows = trailing.shape[0] // cols_size
    places = 8

    live = jnp.arange(slots, dtype=jnp.int32) < group_size[0]
    target = slot_row // sub_rows
    hits = ((target[:, None] == jnp.arange(devices, dtype=jnp.int32)[None, :]) & live[:, None]).astype(BF16)
    earlier = (
        lax.broadcasted_iota(jnp.int32, (slots, slots), 0) > lax.broadcasted_iota(jnp.int32, (slots, slots), 1)
    ).astype(BF16)
    rank = jnp.sum(dot(earlier, hits) * hits.astype(F32), axis=1).astype(jnp.int32)
    place = jnp.where(live, target * places + rank, -1)
    sends = lax.broadcasted_iota(jnp.int32, (devices * places, slots), 0) == place[None, :]
    local = jnp.sum(jnp.where(sends, (slot_row % sub_rows + 1)[None, :], 0), axis=1)
    note = jnp.pad(local.reshape(devices, places).astype(F32), ((0, 0), (0, 128 - places)))[:, None, :]
    note = jnp.where(jnp.arange(places)[None, :, None] == places - 1, note, 0.0).reshape(devices * places, 128)

    own_values = lax.dynamic_slice_in_dim(panel_blocks, device_id * own, own, 0).reshape(own, BS, BS)
    first = jnp.full((1,), device_id * own, jnp.int32)
    ps_rows = panel_call(first, panel_pos, x_mat, y_inv, own_values, panel_blocks)
    ps = lax.all_gather(ps_rows, AXES, axis=0, tiled=True)

    at = group_blocks[device_id]
    send = rows_call(
        panel_pos, at, x_mat, y_inv, panel_blocks, slot_block[:, None], place[None, :], note, cons_blocks
    )
    recv = lax.all_to_all(send.reshape(devices, places, panel_cols), AXES, 0, 0, tiled=True)
    inverse = factor_call(ps)
    local = recv[:, places - 1, :places].astype(jnp.int32).reshape(1, -1) - 1
    slab, slab_high = finish_call(local, recv.reshape(devices * places, panel_cols), inverse, sub_rows)

    block_rows = trailing.shape[1] // rows_size
    lead = slab_high[: block_rows * cols_size].reshape(cols_size, block_rows, panel_cols)
    lead = lax.all_to_all(lead, "col", 0, 0, tiled=True)[0]
    picked = lax.all_to_all(jnp.broadcast_to(lead[None], (rows_size, block_rows, panel_cols)), "row", 0, 0, tiled=True)
    picked = picked.reshape(trailing.shape[1], panel_cols)
    all_rows = lax.all_gather(slab_high, "col", axis=0, tiled=True)
    updated = trailing - dot(all_rows, picked, NT)
    return (slab, updated)


def solution(mesh):
    return jax.shard_map(
        body,
        mesh=mesh,
        in_specs=(
            P(),
            P(),
            P(),
            P(),
            P(),
            P(("row", "col"), None),
            P(("row", "col")),
            P(("row", "col")),
            P(("row", "col")),
            P("row", "col"),
        ),
        out_specs=(P(("row", "col"), None), P("row", "col")),
        check_vma=False,
    )
```
